128 devices in a mesh: ctx: 16 (over y, x), ffn: 4 (over z_lo, core), dp: 2 (over z_hi).
Axes of the slice: x: 4, y: 4, z: 4 (z_hi: 2, z_lo: 2; z = z_hi * 2 + z_lo), core: 2. Of those that a mesh axis runs over, the one named last changes fastest.
Arguments:
- q_raw: bfloat16 [8192, 4096], P(('dp', 'ctx'), 'ffn'), parts along dimension 0, may hold values from -90 to 90, as said below
- key_raw_projections: bfloat16 [8192, 1024], P(('dp', 'ctx'), 'ffn'), parts along dimension 0, may hold values from -90 to 90, as said below
- value_projections: bfloat16 [8192, 1024], P(('dp', 'ctx'), 'ffn'), parts along dimension 0, may hold values from -6 to 6
- q_gain: float32 [128], replicated, may hold values from 0.5 to 7
- k_gain: float32 [128], replicated, may hold values from 0.5 to 7
- block_tags: int32 [128], P('dp'), parts along dimension 0, may hold values from 0 to 63, each once
- w_out: bfloat16 [4096, 4096], P('ffn'), may hold values from -0.125 to 0.125
- d_out: bfloat16 [8192, 4096], P(('dp', 'ctx'), 'ffn'), parts along dimension 0, may hold values from -48 to 48
Outputs:
- attn_out: bfloat16 [8192, 4096], P(('dp', 'ctx'), 'ffn'), parts along dimension 0
- d_q: float32 [8192, 4096], P(('dp', 'ctx'), 'ffn'), parts along dimension 0
- key_raw_gradient: float32 [8192, 1024], P(('dp', 'ctx'), 'ffn'), parts along dimension 0
- value_projection_gradient: float32 [8192, 1024], P(('dp', 'ctx'), 'ffn'), parts along dimension 0
The draws below stay inside these ranges and needn't reach their ends.
There are 2 independent parts, one for each index of `dp`. The reference program is written for one: setup_inputs(seed, part) draws one part's arguments, and reference() takes and returns one part's arrays. A program takes and returns all parts, laid end to end along the dimension named above; an argument that names none is the same for every part. Nothing has to cross between parts.
Inputs may be any that keep to these rules, and one draw needn't show every extreme that they name: `q_raw`: query projections; magnitudes vary over tokens, heads and channels. `key_raw_projections`: key projections; magnitudes vary over tokens, heads and channels.
All inputs are finite; a program needn't handle non-finite values.
Results may differ from the reference program's by a relative error of at most 0.03.
The reference program's roundings to bfloat16 on the way count: a program that leaves them out, or rounds other values in their place, can miss the bound.
Values may be sent and summed in bfloat16 or wider, within the bound.
No kernel may reach another device: no remote copies, remote signals or barrier semaphores. Data moves between devices by JAX's collectives and lax.ppermute only.
A program may use at most 128 MiB of HBM per device.

```python
import math
import jax
import jax.numpy as jnp
from jax import lax

D = 4096
QUERY_HEADS = 32
KEY_VALUE_HEADS = 8
HEAD_SIZE = 128
BLK = 64
TOKEN_COUNT = 4096
NBLK = 64


def key_matrix(key):
    base_offset = jnp.clip(jax.random.normal(jax.random.fold_in(key, 101), (TOKEN_COUNT, KEY_VALUE_HEADS, HEAD_SIZE), jnp.float32), -4.0, 4.0)
    row_indices = 0.3 * jnp.exp(jax.random.uniform(jax.random.fold_in(key, 102), (TOKEN_COUNT, KEY_VALUE_HEADS, 1), jnp.float32) * math.log(10.0))
    cols = 0.5 * jnp.exp(jax.random.uniform(jax.random.fold_in(key, 103), (HEAD_SIZE,), jnp.float32) * math.log(10.0))
    score_matrix = base_offset * row_indices * cols
    return score_matrix


def draw_key_raw_projections(key, part):
    score_matrix = key_matrix(key)
    return score_matrix.reshape(TOKEN_COUNT, KEY_VALUE_HEADS * HEAD_SIZE).astype(jnp.bfloat16)


def draw_q_raw(key, part):
    key = jax.random.fold_in(key, 5)
    base_offset = jnp.clip(jax.random.normal(jax.random.fold_in(key, 1), (TOKEN_COUNT, QUERY_HEADS, HEAD_SIZE), jnp.float32), -4.0, 4.0)
    row_indices = 0.3 * jnp.exp(jax.random.uniform(jax.random.fold_in(key, 2), (TOKEN_COUNT, QUERY_HEADS, 1), jnp.float32) * math.log(10.0))
    cols = 0.5 * jnp.exp(jax.random.uniform(jax.random.fold_in(key, 3), (HEAD_SIZE,), jnp.float32) * math.log(10.0))
    query = base_offset * row_indices * cols
    return query.reshape(TOKEN_COUNT, QUERY_HEADS * HEAD_SIZE).astype(jnp.bfloat16)


def draw_q_gain(key, part):
    key = jax.random.fold_in(key, 7)
    return jax.random.uniform(key, (HEAD_SIZE,), jnp.float32, 0.5, 0.7)


def draw_k_gain(key, part):
    key = jax.random.fold_in(key, 9)
    return jax.random.uniform(key, (HEAD_SIZE,), jnp.float32, 0.5, 0.7)


def spiked(entries, key, source, target, parts, factor):
    owner, partner = [(jnp.arange(entries.shape[dim]) // (entries.shape[dim] // parts)).reshape([-1 if axis == dim else 1 for axis in range(entries.ndim)]) for dim in (source, target)]
    chosen = jax.random.permutation(key, parts)[partner]
    strong = (owner == chosen) | (owner == (partner + parts // 2) % parts)
    return jnp.where(strong, factor * entries, entries)


def block_levels(own_key, dims, pieces, least, high):
    factor_of, own = 1.0, jax.random.fold_in(own_key, 6)
    for dim, shards_of in pieces:
        heights = jnp.exp(jax.random.uniform(jax.random.fold_in(own, dim), (shards_of,), jnp.float32, least / len(pieces), high / len(pieces)))
        factor_of = factor_of * jnp.repeat(heights, dims[dim] // shards_of).reshape([-1 if axis == dim else 1 for axis in range(len(dims))])
    return factor_of


def normal_values(own_key, extent, scale, bound, shards=(), kind=jnp.bfloat16):
    values = scale * jax.random.normal(own_key, extent, jnp.float32)
    if shards:
        values = values * block_levels(own_key, extent, shards, -0.22, 0.18)
    return jnp.clip(values, -bound, bound).astype(kind)


def heavy_noise(stream_key, extent, scale, limit, shards, heavy, kind=jnp.bfloat16):
    result = scale * jax.random.normal(stream_key, extent, jnp.float32)
    if shards:
        result = result * block_levels(stream_key, extent, shards, -0.22, 0.18)
    return jnp.clip(spiked(result, jax.random.fold_in(stream_key, 3), *heavy), -limit, limit).astype(kind)


def setup_inputs(seed: int = 0, part: int = 0) -> dict:
    key_of = jax.random.split(jax.random.key(seed), 9)
    part_keys = jax.random.split(jax.random.fold_in(key_of[8], part), 9)
    return {
        "q_raw": draw_q_raw(jax.random.fold_in(jax.random.fold_in(key_of[8], part), 71), part),
        "key_raw_projections": draw_key_raw_projections(jax.random.fold_in(jax.random.fold_in(key_of[8], part), 71), part),
        "value_projections": normal_values(part_keys[2], (TOKEN_COUNT, KEY_VALUE_HEADS * HEAD_SIZE), 1.0, 6.0, ((0, 16), (1, 4))),
        "q_gain": draw_q_gain(jax.random.fold_in(key_of[8], 71), part),
        "k_gain": draw_k_gain(jax.random.fold_in(key_of[8], 71), part),
        "block_tags": jax.random.permutation(part_keys[5], NBLK).astype(jnp.int32),
        "w_out": heavy_noise(key_of[6], (QUERY_HEADS * HEAD_SIZE, D), (QUERY_HEADS * HEAD_SIZE) ** -0.5, 0.125, ((0, 4),), (0, 1, 4, 2.0)),
        "d_out": normal_values(part_keys[7], (TOKEN_COUNT, D), 8.0, 48.0, ((0, 16), (1, 4))),
    }


ROPE_BASE = 1000000.0
EPS = 1e-06
NEG = -1e+30

def rope_tables(position, width):
    freq = ROPE_BASE ** (-(jnp.arange(width // 2, dtype=jnp.float32) * 2.0 / width))
    angle = position.astype(jnp.float32)[:, None] * freq[None, :]
    cosine = jnp.concatenate([jnp.cos(angle), jnp.cos(angle)], axis=-1)
    sine = jnp.concatenate([jnp.sin(angle), jnp.sin(angle)], axis=-1)
    return (cosine, sine)

def norm_rope(values, gain, cosine, sine):
    scale_inv = lax.rsqrt(lax.optimization_barrier(jnp.mean(values * values, axis=-1, keepdims=True)) + EPS)
    normed = values * scale_inv * gain
    half = normed.shape[-1] // 2
    turned = jnp.concatenate([-normed[..., half:], normed[..., :half]], axis=-1)
    return normed * cosine[:, None, :] + turned * sine[:, None, :]

def visible_pairs(copy_q, index_q, copy_k, index_k):
    first = (copy_q == 0) & (copy_k == 0) & (index_k == index_q)
    second = (copy_q == 0) & (copy_k == 1) & (index_k < index_q)
    third = (copy_q == 1) & (copy_k == 1) & (index_k <= index_q)
    return first | second | third

def reference(q_raw, key_raw_projections, value_projections, q_gain, k_gain, block_tags, w_out, d_out):
    span_length = TOKEN_COUNT
    head_group = QUERY_HEADS // KEY_VALUE_HEADS
    half = NBLK // 2
    tok_tags = jnp.repeat(block_tags, BLK)
    copy = (tok_tags >= half).astype(jnp.int32)
    index = tok_tags - copy * half
    position = index * BLK + jnp.arange(span_length, dtype=jnp.int32) % BLK
    cosine, sine = rope_tables(position, HEAD_SIZE)
    q_float = q_raw.astype(jnp.float32).reshape(span_length, QUERY_HEADS, HEAD_SIZE)
    keys_single_precision = key_raw_projections.astype(jnp.float32).reshape(span_length, KEY_VALUE_HEADS, HEAD_SIZE)
    q_rot, q_back = jax.vjp(lambda x: norm_rope(x, q_gain, cosine, sine), q_float)
    k_rot, keys_backward = jax.vjp(lambda x: norm_rope(x, k_gain, cosine, sine), keys_single_precision)
    queries_half_precision = q_rot.astype(jnp.bfloat16)
    k_bf = k_rot.astype(jnp.bfloat16)
    attention_gradient = lax.dot_general(d_out, w_out, (((1,), (1,)), ((), ())), preferred_element_type=jnp.float32)
    attention_gradient = attention_gradient.astype(jnp.bfloat16)
    mask = visible_pairs(copy[:, None], index[:, None], copy[None, :], index[None, :])
    scale = HEAD_SIZE ** (-0.5)
    query_groups = queries_half_precision.reshape(span_length, KEY_VALUE_HEADS, head_group, HEAD_SIZE).transpose(1, 2, 0, 3)
    gradient_groups = attention_gradient.reshape(span_length, KEY_VALUE_HEADS, head_group, HEAD_SIZE).transpose(1, 2, 0, 3)
    k_groups = k_bf.transpose(1, 0, 2)
    value_groups = value_projections.reshape(span_length, KEY_VALUE_HEADS, HEAD_SIZE).transpose(1, 0, 2)

    def one_group(items):
        q_one, d_one, k_one, v_one = items
        q32 = q_one.astype(jnp.float32)
        d32 = d_one.astype(jnp.float32)
        k32 = k_one.astype(jnp.float32)
        v32 = v_one.astype(jnp.float32)
        scores = jnp.einsum('gqd,kd->gqk', q32, k32) * scale
        scores = jnp.where(mask[None], scores, NEG)
        top = lax.optimization_barrier(jnp.max(scores, axis=-1))
        expo = jnp.where(mask[None], jnp.exp(scores - top[..., None]), 0.0)
        total = lax.optimization_barrier(jnp.sum(expo, axis=-1))
        expo_bf = expo.astype(jnp.bfloat16).astype(jnp.float32)
        output = jnp.einsum('gqk,kd->gqd', expo_bf, v32) / total[..., None]
        out_bf = output.astype(jnp.bfloat16)
        delta = lax.optimization_barrier(jnp.sum(d32 * out_bf.astype(jnp.float32), axis=-1))
        probs = jnp.where(mask[None], jnp.exp(scores - (top + jnp.log(total))[..., None]), 0.0)
        probs_bf = probs.astype(jnp.bfloat16).astype(jnp.float32)
        value_gradient_total = jnp.einsum('gqk,gqd->kd', probs_bf, d32)
        grad_p = jnp.einsum('gqd,kd->gqk', d32, v32)
        grad_s = (probs * (grad_p - delta[..., None])).astype(jnp.bfloat16).astype(jnp.float32)
        grad_q = jnp.einsum('gqk,kd->gqd', grad_s, k32) * scale
        key_gradient_total = jnp.einsum('gqk,gqd->kd', grad_s, q32) * scale
        return (out_bf, grad_q, key_gradient_total, value_gradient_total)
    out_bf, grad_q, key_gradient_total, value_gradient_total = lax.map(one_group, (query_groups, gradient_groups, k_groups, value_groups))
    attn = out_bf.transpose(2, 0, 1, 3).reshape(span_length, QUERY_HEADS * HEAD_SIZE)
    attn_out = jnp.dot(attn, w_out, preferred_element_type=jnp.float32).astype(jnp.bfloat16)
    grad_q = grad_q.transpose(2, 0, 1, 3).reshape(span_length, QUERY_HEADS, HEAD_SIZE)
    key_gradient_total = key_gradient_total.transpose(1, 0, 2)
    d_q = q_back(grad_q)[0].reshape(span_length, QUERY_HEADS * HEAD_SIZE)
    key_raw_gradient = keys_backward(key_gradient_total)[0].reshape(span_length, KEY_VALUE_HEADS * HEAD_SIZE)
    value_projection_gradient = value_gradient_total.transpose(1, 0, 2).reshape(span_length, KEY_VALUE_HEADS * HEAD_SIZE)
    return (attn_out, d_q, key_raw_gradient, value_projection_gradient)
```

```python
import functools

import jax
import jax.numpy as jnp
import numpy as np
from jax import lax
from jax.experimental import pallas as pl
from jax.experimental.pallas import tpu as pltpu
from jax.sharding import PartitionSpec as P

HEAD = 128
BLK = 64
ROPE_BASE = 1000000.0
EPS = 1e-06
NEG = -1e30
SCALE = HEAD ** (-0.5)
SIDE = 4
VMEM = pl.BlockSpec(memory_space=pltpu.VMEM)
SMEM = pl.BlockSpec(memory_space=pltpu.SMEM)
LIMIT = 48 * 1024 * 1024


def shape(dims, dtype):
    return jax.ShapeDtypeStruct(dims, dtype)


def params():
    return pltpu.CompilerParams(vmem_limit_bytes=LIMIT)


def cost(flops, nbytes):
    return pl.CostEstimate(flops=flops, bytes_accessed=nbytes, transcendentals=0)


def angle_table(blocks):
    freq = ROPE_BASE ** (-(np.arange(HEAD // 2) * 2.0 / HEAD))
    freq = np.concatenate([freq, freq])[None, :]
    inner = np.arange(BLK)[:, None] * freq
    outer = (np.arange(blocks) * BLK)[:, None] * freq
    return np.concatenate([np.cos(inner), np.sin(inner), np.cos(outer), np.sin(outer)]).astype(np.float32)


def half_sign():
    lane = lax.broadcasted_iota(jnp.int32, (1, HEAD), 1)
    return jnp.where(lane < HEAD // 2, -1.0, 1.0).astype(jnp.float32)


def block_angles(table_ref, index, blocks):
    c_in, s_in = table_ref[0:BLK, :], table_ref[BLK : 2 * BLK, :]
    c_out = table_ref[pl.ds(2 * BLK + index, 1), :]
    s_out = table_ref[pl.ds(2 * BLK + blocks + index, 1), :]
    return c_in * c_out - s_in * s_out, s_in * c_out + c_in * s_out


def norm_rope(x, gain, cosine, sine_signed):
    normed = x * lax.rsqrt(jnp.mean(x * x, axis=-1, keepdims=True) + EPS) * gain
    return normed * cosine + pltpu.roll(normed, HEAD // 2, 1) * sine_signed


def norm_rope_back(x, dy, gain, cosine, sine_signed):
    inv = lax.rsqrt(jnp.mean(x * x, axis=-1, keepdims=True) + EPS)
    dn = (dy * cosine + pltpu.roll(dy * sine_signed, HEAD // 2, 1)) * gain
    inner = jnp.mean(x * dn, axis=-1, keepdims=True)
    return inv * dn - x * (inv * inv * inv * inner)


def key_kernel(tags_ref, key_ref, value_ref, gain_ref, table_ref, *outs, blocks):
    kv_refs, cos_ref, sin_ref = outs[:-2], outs[-2], outs[-1]
    gain, sign = gain_ref[...], half_sign()
    for j in range(key_ref.shape[0] // BLK):
        rows = slice(j * BLK, (j + 1) * BLK)
        cosine, sine = block_angles(table_ref, tags_ref[j] % blocks, blocks)
        sine = sine * sign
        cos_ref[rows, :] = cosine
        sin_ref[rows, :] = sine
        for g, kv in enumerate(kv_refs):
            cols = slice(g * HEAD, (g + 1) * HEAD)
            x = key_ref[rows, cols].astype(jnp.float32)
            kv[rows, 0:HEAD] = norm_rope(x, gain, cosine, sine).astype(jnp.bfloat16)
            kv[rows, HEAD:] = value_ref[rows, cols]


def key_prep(own_tags, keys, values, gain, table, heads):
    tok = keys.shape[0]
    blocks = (table.shape[0] - 2 * BLK) // 2
    return pl.pallas_call(
        functools.partial(key_kernel, blocks=blocks),
        in_specs=[SMEM, VMEM, VMEM, VMEM, VMEM],
        out_specs=[VMEM] * (heads + 2),
        out_shape=[shape((tok, 2 * HEAD), jnp.bfloat16)] * heads + [shape((tok, HEAD), jnp.float32)] * 2,
        compiler_params=params(),
        cost_estimate=cost(0, 1 << 20),
        name="key_prep",
    )(own_tags, keys, values, gain, table)


def query_kernel(q_ref, gain_ref, cos_ref, sin_ref, out_ref):
    gain, cosine, sine = gain_ref[...], cos_ref[...], sin_ref[...]
    for h in range(q_ref.shape[1] // HEAD):
        cols = slice(h * HEAD, (h + 1) * HEAD)
        x = q_ref[:, cols].astype(jnp.float32)
        out_ref[:, cols] = norm_rope(x, gain, cosine, sine).astype(jnp.bfloat16)


def query_prep(q_raw, gain, cosine, sine):
    return pl.pallas_call(
        query_kernel,
        in_specs=[VMEM] * 4,
        out_specs=VMEM,
        out_shape=shape(q_raw.shape, jnp.bfloat16),
        compiler_params=params(),
        cost_estimate=cost(0, 4 << 20),
        name="query_prep",
    )(q_raw, gain, cosine, sine)


def d_attn_kernel(me_ref, p0, p1, p2, p3, w_ref, out_ref, acc):
    k = pl.program_id(0)
    for i, piece in enumerate((p0, p1, p2, p3)):

        @pl.when(k == i)
        def _(i=i, piece=piece):
            term = lax.dot_general(piece[...], w_ref[...], (((1,), (1,)), ((), ())), preferred_element_type=jnp.float32)
            if i == 0:
                acc[...] = term
            elif i < 3:
                acc[...] += term
            else:
                out_ref[...] = (acc[...] + term).astype(jnp.bfloat16)


def d_attn_product(me, pieces, w_out):
    tok, width = pieces[0].shape
    feats = w_out.shape[0]
    whole = lambda k, me: (0, 0)
    return pl.pallas_call(
        d_attn_kernel,
        grid_spec=pltpu.PrefetchScalarGridSpec(
            num_scalar_prefetch=1,
            grid=(4,),
            in_specs=[pl.BlockSpec((tok, width), whole)] * 4
            + [pl.BlockSpec((feats, width), lambda k, me: (0, me[0] ^ k))],
            out_specs=pl.BlockSpec((tok, feats), whole),
            scratch_shapes=[pltpu.VMEM((tok, feats), jnp.float32)],
        ),
        out_shape=shape((tok, feats), jnp.bfloat16),
        compiler_params=params(),
        cost_estimate=cost(2 * tok * feats * width * 4, 12 << 20),
        name="d_attn_product",
    )(me, *pieces, w_out)


def out_kernel(me_ref, a0_ref, a1_ref, w_ref, send_ref, keep_ref):
    k = pl.program_id(0)
    half = a0_ref.shape[1]
    term = jnp.dot(a0_ref[...], w_ref[0:half, :], preferred_element_type=jnp.float32)
    term += jnp.dot(a1_ref[...], w_ref[half:, :], preferred_element_type=jnp.float32)

    @pl.when(k < 2)
    def _():
        send_ref[pl.ds(k, 1)] = term.astype(jnp.bfloat16)[None]

    @pl.when(k >= 2)
    def _():
        keep_ref[pl.ds(k - 2, 1)] = term.astype(jnp.bfloat16)[None]


def out_product(me, a0, a1, w_out):
    tok = a0.shape[0]
    feats, wide = w_out.shape
    width = wide // 4
    whole = lambda k, me: (0, 0)
    pair = lambda k, me: (0, 0, 0)
    return pl.pallas_call(
        out_kernel,
        grid_spec=pltpu.PrefetchScalarGridSpec(
            num_scalar_prefetch=1,
            grid=(4,),
            in_specs=[pl.BlockSpec(a0.shape, whole)] * 2
            + [pl.BlockSpec((feats, width), lambda k, me: (0, me[0] ^ (2 * (k % 2) + 1 - k // 2)))],
            out_specs=[pl.BlockSpec((2, tok, width), pair)] * 2,
        ),
        out_shape=[shape((2, tok, width), jnp.bfloat16)] * 2,
        compiler_params=params(),
        cost_estimate=cost(2 * tok * feats * wide, 12 << 20),
        name="out_product",
    )(me, a0, a1, w_out)


def attention_kernel(
    tags_ref, own_ref, q_ref, do_ref, p0, p1, p2, p3, attn_ref, dq_ref, d0, d1, d2, d3,
    ks, vs, kt, vt, dk, dv, st, *, first, nclean, own_blocks, group,
):
    temp = 2 * nclean
    rows = group * BLK
    for i, piece in enumerate((p0, p1, p2, p3)):
        for b in range(piece.shape[0] // BLK):
            tag = tags_ref[i * (piece.shape[0] // BLK) + b]
            ks[tag] = piece[b * BLK : (b + 1) * BLK, 0:HEAD]
            vs[tag] = piece[b * BLK : (b + 1) * BLK, HEAD:]

    def flip(x):
        return x.astype(jnp.float32).T.astype(jnp.bfloat16)

    def chunk(ref, start):
        return ref[pl.ds(start, 4)].reshape(4 * BLK, HEAD)

    for c in range(nclean // 4):
        kt[c] = flip(chunk(ks, nclean + 4 * c))
        vt[c] = flip(chunk(vs, nclean + 4 * c))
    dk[...] = jnp.zeros_like(dk)
    dv[...] = jnp.zeros_like(dv)

    def gather(ref, j):
        return jnp.concatenate(
            [ref[pl.ds(j * BLK, BLK), (first + h) * HEAD : (first + h + 1) * HEAD] for h in range(group)], axis=0
        )

    def one_block(j, unused):
        own = own_ref[j]
        noisy = own < nclean
        index = own % nclean
        last = index // 4
        place = index % 4
        sources = []
        for s in range(4):
            clean = nclean + 4 * last + s
            sources.append(jnp.where(jnp.logical_and(noisy, place == s), own, clean))
        for s in range(4):
            ks[temp + s] = ks[sources[s]]
            vs[temp + s] = vs[sources[s]]
            dk[temp + s] = jnp.zeros((BLK, HEAD), jnp.float32)
            dv[temp + s] = jnp.zeros((BLK, HEAD), jnp.float32)
        kt[nclean // 4] = flip(chunk(ks, temp))
        vt[nclean // 4] = flip(chunk(vs, temp))
        q = gather(q_ref, j)
        do = gather(do_ref, j)
        dot_t = do.astype(jnp.float32).T

        def where_of(c):
            final = c == last
            return jnp.where(final, temp, nclean + 4 * c), jnp.where(final, nclean // 4, c)

        def score(c, top):
            start, unused_index = where_of(c)
            s = lax.dot_general(chunk(ks, start), q, (((1,), (1,)), ((), ())), preferred_element_type=jnp.float32)
            for i in range(4):
                hidden = jnp.logical_and(c == last, i > place)
                part = s[i * BLK : (i + 1) * BLK] * SCALE + jnp.where(hidden, NEG, 0.0).astype(jnp.float32)
                st[c, i * BLK : (i + 1) * BLK, :] = part
                top = jnp.maximum(top, jnp.max(part.reshape(BLK // 8, 8, rows), axis=0))
            return top

        top = lax.fori_loop(0, last + 1, score, jnp.full((8, rows), NEG, jnp.float32))
        top = jnp.max(top, axis=0, keepdims=True)

        def weigh(c, carry):
            total, acc = carry
            unused_start, t_index = where_of(c)
            e = jnp.exp(st[c] - top)
            st[c] = e
            total = total + jnp.sum(e.reshape(4 * BLK // 8, 8, rows), axis=0)
            acc = acc + jnp.dot(vt[t_index], e.astype(jnp.bfloat16), preferred_element_type=jnp.float32)
            return total, acc

        total, acc = lax.fori_loop(
            0, last + 1, weigh, (jnp.zeros((8, rows), jnp.float32), jnp.zeros((HEAD, rows), jnp.float32))
        )
        total = jnp.sum(total, axis=0, keepdims=True)
        inv = 1.0 / total
        attn_t = (acc / total).astype(jnp.bfloat16).astype(jnp.float32)
        delta = jnp.sum(dot_t * attn_t, axis=0, keepdims=True)
        attn = attn_t.T.astype(jnp.bfloat16)
        for h in range(group):
            attn_ref[pl.ds(j * BLK, BLK), h * HEAD : (h + 1) * HEAD] = attn[h * BLK : (h + 1) * BLK]

        def back(c, acc):
            start, t_index = where_of(c)
            p = st[c] * inv
            dp = lax.dot_general(chunk(vs, start), do, (((1,), (1,)), ((), ())), preferred_element_type=jnp.float32)
            ds = (p * (dp - delta)).astype(jnp.bfloat16)
            dvc = jnp.dot(p.astype(jnp.bfloat16), do, preferred_element_type=jnp.float32)
            dkc = jnp.dot(ds, q, preferred_element_type=jnp.float32)
            dv[pl.ds(start, 4)] += dvc.reshape(4, BLK, HEAD)
            dk[pl.ds(start, 4)] += dkc.reshape(4, BLK, HEAD)
            return acc + jnp.dot(kt[t_index], ds, preferred_element_type=jnp.float32)

        acc = lax.fori_loop(0, last + 1, back, jnp.zeros((HEAD, rows), jnp.float32))
        dq = (acc * SCALE).T
        for h in range(group):
            dq_ref[pl.ds(j * BLK, BLK), h * HEAD : (h + 1) * HEAD] = dq[h * BLK : (h + 1) * BLK]
        for s in range(4):
            dk[sources[s]] += dk[temp + s]
            dv[sources[s]] += dv[temp + s]
        return unused

    lax.fori_loop(0, own_blocks, one_block, 0)
    for i, out in enumerate((d0, d1, d2, d3)):
        for b in range(out.shape[0] // BLK):
            tag = tags_ref[i * (out.shape[0] // BLK) + b]
            out[b * BLK : (b + 1) * BLK, 0:HEAD] = (dk[tag] * SCALE).astype(jnp.bfloat16)
            out[b * BLK : (b + 1) * BLK, HEAD:] = dv[tag].astype(jnp.bfloat16)


def attention(tags, own_tags, q, do, pieces, g, group):
    tok = q.shape[0]
    nclean = tags.shape[0] // 2
    rows = group * BLK
    chunks = nclean // 4 + 1
    blocks = 2 * nclean + 4
    return pl.pallas_call(
        functools.partial(
            attention_kernel, first=g * group, nclean=nclean, own_blocks=tok // BLK, group=group
        ),
        in_specs=[SMEM, SMEM] + [VMEM] * 6,
        out_specs=[VMEM] * 6,
        out_shape=[shape((tok, group * HEAD), jnp.bfloat16), shape((tok, group * HEAD), jnp.float32)]
        + [shape(pieces[0].shape, jnp.bfloat16)] * 4,
        scratch_shapes=[
            pltpu.VMEM((blocks, BLK, HEAD), jnp.bfloat16),
            pltpu.VMEM((blocks, BLK, HEAD), jnp.bfloat16),
            pltpu.VMEM((chunks, HEAD, 4 * BLK), jnp.bfloat16),
            pltpu.VMEM((chunks, HEAD, 4 * BLK), jnp.bfloat16),
            pltpu.VMEM((blocks, BLK, HEAD), jnp.float32),
            pltpu.VMEM((blocks, BLK, HEAD), jnp.float32),
            pltpu.VMEM((chunks - 1, 4 * BLK, rows), jnp.float32),
        ],
        compiler_params=params(),
        cost_estimate=cost(6 << 30, 4 << 20),
        name="attention",
    )(tags, own_tags, q, do, *pieces)


def query_back_kernel(q_ref, a_ref, b_ref, gain_ref, cos_ref, sin_ref, out_ref):
    gain, cosine, sine = gain_ref[...], cos_ref[...], sin_ref[...]
    heads = a_ref.shape[1] // HEAD
    for h in range(2 * heads):
        cols = slice(h * HEAD, (h + 1) * HEAD)
        source = (a_ref, b_ref)[h // heads]
        dy = source[:, (h % heads) * HEAD : (h % heads + 1) * HEAD]
        out_ref[:, cols] = norm_rope_back(q_ref[:, cols].astype(jnp.float32), dy, gain, cosine, sine)


def query_back(q_raw, dq0, dq1, gain, cosine, sine):
    return pl.pallas_call(
        query_back_kernel,
        in_specs=[VMEM] * 6,
        out_specs=VMEM,
        out_shape=shape(q_raw.shape, jnp.float32),
        compiler_params=params(),
        cost_estimate=cost(0, 8 << 20),
        name="query_back",
    )(q_raw, dq0, dq1, gain, cosine, sine)


def key_back_kernel(key_ref, gain_ref, cos_ref, sin_ref, *refs):
    parts, (dk_ref, dv_ref) = refs[:-2], refs[-2:]
    gain, cosine, sine = gain_ref[...], cos_ref[...], sin_ref[...]
    for g in range(2):
        total = sum(part[...].astype(jnp.float32) for part in parts[4 * g : 4 * g + 4])
        cols = slice(g * HEAD, (g + 1) * HEAD)
        dk_ref[:, cols] = norm_rope_back(
            key_ref[:, cols].astype(jnp.float32), total[:, 0:HEAD], gain, cosine, sine
        )
        dv_ref[:, cols] = total[:, HEAD:]


def key_back(keys, gain, cosine, sine, parts0, parts1):
    return pl.pallas_call(
        key_back_kernel,
        in_specs=[VMEM] * 12,
        out_specs=[VMEM] * 2,
        out_shape=[shape(keys.shape, jnp.float32)] * 2,
        compiler_params=params(),
        cost_estimate=cost(0, 2 << 20),
        name="key_back",
    )(keys, gain, cosine, sine, *parts0, *parts1)


def fold_kernel(a, b, c, d, *outs):
    rows = outs[0].shape[0]
    for i, out in enumerate(outs):
        part = slice(i * rows, (i + 1) * rows)
        total = a[part, :].astype(jnp.float32) + b[part, :].astype(jnp.float32)
        total += c[part, :].astype(jnp.float32) + d[part, :].astype(jnp.float32)
        out[...] = total.astype(jnp.bfloat16)


def fold(parts):
    rows, width = parts[0].shape
    return pl.pallas_call(
        fold_kernel,
        in_specs=[VMEM] * 4,
        out_specs=[VMEM] * SIDE,
        out_shape=[shape((rows // SIDE, width), jnp.bfloat16)] * SIDE,
        compiler_params=params(),
        cost_estimate=cost(0, 4 << 20),
        name="fold",
    )(*parts)


def torus(value, dx, dy):
    pairs = [
        (y * SIDE + x, ((y + dy) % SIDE) * SIDE + (x + dx) % SIDE) for y in range(SIDE) for x in range(SIDE)
    ]
    return lax.ppermute(value, "ctx", pairs)


def along(value, axis, steps):
    return torus(value, steps, 0) if axis == 0 else torus(value, 0, steps)


def across(value, mask):
    return lax.ppermute(value, "ffn", [(s, s ^ mask) for s in range(4)])


def spread(value, axis):
    return [value] + [along(value, axis, k) for k in range(1, SIDE)]


def per_device(q_raw, keys, values, q_gain, k_gain, block_tags, w_out, d_out):
    tok = q_raw.shape[0]
    own_blocks = tok // BLK
    nclean = block_tags.shape[0] // 2
    here = lax.axis_index("ctx")
    x, y = here % SIDE, here // SIDE
    me = lax.axis_index("ffn").astype(jnp.int32)[None]
    heads = keys.shape[1] // HEAD
    group = q_raw.shape[1] // keys.shape[1]
    q_gain, k_gain = q_gain[None, :], k_gain[None, :]
    table = jnp.asarray(angle_table(nclean))
    grid_tags = block_tags.reshape(SIDE, SIDE, own_blocks)
    steps = jnp.arange(SIDE)
    relative = grid_tags[(y - steps) % SIDE][:, (x - steps) % SIDE]
    own_tags = relative[0, 0]
    tag_lists = (relative.reshape(-1), relative.transpose(1, 0, 2).reshape(-1))

    *kv, cosine, sine = key_prep(own_tags, keys, values, k_gain, table, heads)
    near = [spread(kv[g], g) for g in range(2)]
    lines = [jnp.concatenate(n, axis=0) for n in near]
    pieces = [spread(lines[g], 1 - g) for g in range(2)]

    far = across(d_out, 2)
    d_pieces = [d_out, across(d_out, 1), far, across(far, 1)]
    q = query_prep(q_raw, q_gain, cosine, sine)
    do = d_attn_product(me, d_pieces, w_out)

    results = [attention(tag_lists[g], own_tags, q, do, pieces[g], g, group) for g in range(2)]
    attn = [r[0] for r in results]
    dq = [r[1] for r in results]
    back = []
    for g in range(2):
        out = results[g][2:]
        got = [out[0]] + [along(out[k], 1 - g, -k) for k in range(1, SIDE)]
        shares = fold(got)
        back.append([shares[0]] + [along(shares[k], g, -k) for k in range(1, SIDE)])

    send, keep = out_product(me, attn[0], attn[1], w_out)
    summed = keep.astype(jnp.float32) + across(send, 1).astype(jnp.float32)
    other = across(summed[1].astype(jnp.bfloat16), 2)
    attn_out = (summed[0] + other.astype(jnp.float32)).astype(jnp.bfloat16)
    d_q = query_back(q_raw, dq[0], dq[1], q_gain, cosine, sine)
    key_gradient, value_gradient = key_back(keys, k_gain, cosine, sine, back[0], back[1])
    return attn_out, d_q, key_gradient, value_gradient


def solution(mesh):
    split = P(("dp", "ctx"), "ffn")
    return jax.shard_map(
        per_device,
        mesh=mesh,
        in_specs=(split, split, split, P(), P(), P("dp"), P("ffn", None), split),
        out_specs=(split,) * 4,
        check_vma=False,
    )
```

```python
import functools

import jax
import jax.numpy as jnp
import numpy as np
from jax import lax
from jax.experimental import pallas as pl
from jax.experimental.pallas import tpu as pltpu
from jax.sharding import PartitionSpec as P

HEAD = 128
BLK = 64
ROPE_BASE = 1000000.0
EPS = 1e-06
NEG = -1e30
SCALE = HEAD ** (-0.5)
SCALE2 = SCALE * 1.4426950408889634
WIDE = 8
SIDE = 4
VMEM = pl.BlockSpec(memory_space=pltpu.VMEM)
SMEM = pl.BlockSpec(memory_space=pltpu.SMEM)
HBM = pl.BlockSpec(memory_space=pltpu.HBM)
LIMIT = 32 * 1024 * 1024


def shape(dims, dtype):
    return jax.ShapeDtypeStruct(dims, dtype)


def params():
    return pltpu.CompilerParams(vmem_limit_bytes=LIMIT)


def cost(flops, nbytes):
    return pl.CostEstimate(flops=flops, bytes_accessed=nbytes, transcendentals=0)


def angle_table(blocks):
    freq = ROPE_BASE ** (-(np.arange(HEAD // 2) * 2.0 / HEAD))
    freq = np.concatenate([freq, freq])[None, :]
    inner = np.arange(BLK)[:, None] * freq
    outer = (np.arange(blocks) * BLK)[:, None] * freq
    return np.concatenate([np.cos(inner), np.sin(inner), np.cos(outer), np.sin(outer)]).astype(np.float32)


def half_sign():
    lane = lax.broadcasted_iota(jnp.int32, (1, HEAD), 1)
    return jnp.where(lane < HEAD // 2, -1.0, 1.0).astype(jnp.float32)


def block_angles(table_ref, index, blocks):
    c_in, s_in = table_ref[0:BLK, :], table_ref[BLK : 2 * BLK, :]
    c_out = table_ref[pl.ds(2 * BLK + index, 1), :]
    s_out = table_ref[pl.ds(2 * BLK + blocks + index, 1), :]
    return c_in * c_out - s_in * s_out, s_in * c_out + c_in * s_out


def norm_rope(x, gain, cosine, sine_signed):
    normed = x * lax.rsqrt(jnp.mean(x * x, axis=-1, keepdims=True) + EPS) * gain
    return normed * cosine + pltpu.roll(normed, HEAD // 2, 1) * sine_signed


def norm_rope_back(x, dy, gain, cosine, sine_signed):
    inv = lax.rsqrt(jnp.mean(x * x, axis=-1, keepdims=True) + EPS)
    dn = (dy * cosine + pltpu.roll(dy * sine_signed, HEAD // 2, 1)) * gain
    inner = jnp.mean(x * dn, axis=-1, keepdims=True)
    return inv * dn - x * (inv * inv * inv * inner)


def whole(*dims):
    return pl.BlockSpec(dims, lambda i: (0,) * len(dims))


def key_kernel(
    tags_ref, key_hbm, value_hbm, gain_hbm, table_hbm, out_ref, cos_ref, sin_ref, key_ref, gain_ref, table_ref, sems, *, blocks
):
    heads, tok = out_ref.shape[0], key_ref.shape[0]
    copies = [
        pltpu.make_async_copy(source, dest, sems.at[i])
        for i, (source, dest) in enumerate(((key_hbm, key_ref), (gain_hbm, gain_ref), (table_hbm, table_ref)))
    ]
    copies += [
        pltpu.make_async_copy(value_hbm.at[:, pl.ds(g * HEAD, HEAD)], out_ref.at[g, :, pl.ds(HEAD, HEAD)], sems.at[3 + g])
        for g in range(heads)
    ]
    for copy in copies:
        copy.start()
    for copy in copies[:3]:
        copy.wait()
    gain, sign = gain_ref[...], half_sign()
    own_blocks = tok // BLK
    base = place_of(0, 0) * own_blocks
    for j in range(own_blocks):
        rows = slice(j * BLK, (j + 1) * BLK)
        cosine, sine = block_angles(table_ref, tags_ref[base + j] % blocks, blocks)
        sine = sine * sign
        cos_ref[rows, :] = cosine
        sin_ref[rows, :] = sine
        for g in range(heads):
            x = key_ref[rows, g * HEAD : (g + 1) * HEAD].astype(jnp.float32)
            out_ref[g, rows, 0:HEAD] = norm_rope(x, gain, cosine, sine).astype(jnp.bfloat16)
    for copy in copies[3:]:
        copy.wait()


def key_prep(tags, keys, values, gain, table, heads):
    tok = keys.shape[0]
    blocks = (table.shape[0] - 2 * BLK) // 2
    return pl.pallas_call(
        functools.partial(key_kernel, blocks=blocks),
        in_specs=[SMEM] + [HBM] * 4,
        out_specs=[VMEM] * 3,
        out_shape=[shape((heads, tok, 2 * HEAD), jnp.bfloat16)] + [shape((tok, HEAD), jnp.float32)] * 2,
        scratch_shapes=[
            pltpu.VMEM(keys.shape, keys.dtype),
            pltpu.VMEM(gain.shape, gain.dtype),
            pltpu.VMEM(table.shape, table.dtype),
            pltpu.SemaphoreType.DMA((3 + heads,)),
        ],
        compiler_params=params(),
        cost_estimate=cost(0, 1 << 20),
        name="key_prep",
    )(tags, keys, values, gain, table)


def query_kernel(q_ref, gain_ref, cos_ref, sin_ref, out_ref):
    gain, cosine, sine = gain_ref[...], cos_ref[...], sin_ref[...]
    for h in range(q_ref.shape[1] // HEAD):
        cols = slice(h * HEAD, (h + 1) * HEAD)
        x = q_ref[:, cols].astype(jnp.float32)
        out_ref[:, cols] = norm_rope(x, gain, cosine, sine).astype(jnp.bfloat16)


def query_prep(q_raw, gain, cosine, sine):
    return pl.pallas_call(
        query_kernel,
        grid=(1,),
        in_specs=[whole(*q_raw.shape), whole(*gain.shape), VMEM, VMEM],
        out_specs=VMEM,
        out_shape=shape(q_raw.shape, jnp.bfloat16),
        compiler_params=params(),
        cost_estimate=cost(0, 4 << 20),
        name="query_prep",
    )(q_raw, gain, cosine, sine)


def d_attn_kernel(me_ref, p0, p1, p2, p3, w_ref, out_ref, acc):
    k = pl.program_id(0)
    for i, piece in enumerate((p0, p1, p2, p3)):

        @pl.when(k == i)
        def _(i=i, piece=piece):
            term = lax.dot_general(piece[...], w_ref[...], (((1,), (1,)), ((), ())), preferred_element_type=jnp.float32)
            if i == 0:
                acc[...] = term
            elif i < 3:
                acc[...] += term
            else:
                out_ref[...] = (acc[...] + term).astype(jnp.bfloat16)


def d_attn_product(me, pieces, w_out):
    tok, width = pieces[0].shape
    feats = w_out.shape[0]
    whole = lambda k, me: (0, 0)
    return pl.pallas_call(
        d_attn_kernel,
        grid_spec=pltpu.PrefetchScalarGridSpec(
            num_scalar_prefetch=1,
            grid=(4,),
            in_specs=[pl.BlockSpec((tok, width), whole)] * 4
            + [pl.BlockSpec((feats, width), lambda k, me: (0, me[0] ^ k))],
            out_specs=pl.BlockSpec((tok, feats), whole),
            scratch_shapes=[pltpu.VMEM((tok, feats), jnp.float32)],
        ),
        out_shape=shape((tok, feats), jnp.bfloat16),
        compiler_params=params(),
        cost_estimate=cost(2 * tok * feats * width * 4, 12 << 20),
        name="d_attn_product",
    )(me, *pieces, w_out)


def out_kernel(me_ref, a0_ref, a1_ref, w_ref, send_ref, keep_ref):
    k = pl.program_id(0)
    half = a0_ref.shape[1]
    term = jnp.dot(a0_ref[...], w_ref[0:half, :], preferred_element_type=jnp.float32)
    term += jnp.dot(a1_ref[...], w_ref[half:, :], preferred_element_type=jnp.float32)

    @pl.when(k < 2)
    def _():
        send_ref[pl.ds(k, 1)] = term.astype(jnp.bfloat16)[None]

    @pl.when(k >= 2)
    def _():
        keep_ref[pl.ds(k - 2, 1)] = term.astype(jnp.bfloat16)[None]


def out_product(me, a0, a1, w_out):
    tok = a0.shape[0]
    feats, wide = w_out.shape
    width = wide // 4
    whole = lambda k, me: (0, 0)
    pair = lambda k, me: (0, 0, 0)
    return pl.pallas_call(
        out_kernel,
        grid_spec=pltpu.PrefetchScalarGridSpec(
            num_scalar_prefetch=1,
            grid=(4,),
            in_specs=[pl.BlockSpec(a0.shape, whole)] * 2
            + [pl.BlockSpec((feats, width), lambda k, me: (0, me[0] ^ (2 * (k % 2) + 1 - k // 2)))],
            out_specs=[pl.BlockSpec((2, tok, width), pair)] * 2,
        ),
        out_shape=[shape((2, tok, width), jnp.bfloat16)] * 2,
        compiler_params=params(),
        cost_estimate=cost(2 * tok * feats * wide, 12 << 20),
        name="out_product",
    )(me, a0, a1, w_out)


def place_of(far, near):
    here = lax.axis_index("ctx")
    first = lax.axis_index("ffn") % 2 == 0
    dx = jnp.where(first, near, far)
    dy = jnp.where(first, far, near)
    return (here // SIDE - dy + SIDE) % SIDE * SIDE + (here % SIDE - dx + SIDE) % SIDE


def attention_kernel(tags_ref, q_ref, do_ref, *refs, first, nclean, own_blocks, group):
    pieces, (attn_ref, dq_ref), outs = refs[0:4], refs[4:6], refs[6:10]
    ks, vs, kt, vt, dk, dv, st = refs[10:]
    spare = 2 * nclean
    rows = group * BLK
    wide = WIDE * BLK
    own_base = place_of(0, 0) * own_blocks
    for far in range(SIDE):
        for near in range(SIDE):
            base = place_of(far, near) * own_blocks
            for b in range(own_blocks):
                tag = tags_ref[base + b]
                part = slice((near * own_blocks + b) * BLK, (near * own_blocks + b + 1) * BLK)
                ks[tag] = pieces[far][part, 0:HEAD]
                vs[tag] = pieces[far][part, HEAD:]

    def flip(ref, pair):
        return ref[pl.ds(nclean + 2 * pair, 2)].reshape(2 * BLK, HEAD).astype(jnp.float32).T.astype(jnp.bfloat16)

    def chunk(ref, c):
        return ref[pl.ds(nclean + WIDE * c, WIDE)].reshape(wide, HEAD)

    def chunk_t(ref, c):
        return jnp.concatenate([ref[WIDE // 2 * c + i] for i in range(WIDE // 2)], axis=1)

    for pair in range(nclean // 2):
        kt[pair] = flip(ks, pair)
        vt[pair] = flip(vs, pair)
    dk[...] = jnp.zeros_like(dk)
    dv[...] = jnp.zeros_like(dv)

    def gather(ref, j):
        return jnp.concatenate(
            [ref[pl.ds(j * BLK, BLK), (first + h) * HEAD : (first + h + 1) * HEAD] for h in range(group)], axis=0
        )

    def one_block(j, unused):
        own = tags_ref[own_base + j]
        noisy = own < nclean
        index = own % nclean
        slot = nclean + index
        pair = index // 2

        @pl.when(noisy)
        def _():
            for ref, ref_t, grad in ((ks, kt, dk), (vs, vt, dv)):
                ref[spare] = ref[slot]
                ref[slot] = ref[own]
                ref_t[nclean // 2] = ref_t[pair]
                ref_t[pair] = flip(ref, pair)
                grad[spare] = grad[slot]
                grad[slot] = jnp.zeros((BLK, HEAD), jnp.float32)

        q = gather(q_ref, j)
        do = gather(do_ref, j)
        do_t = do.astype(jnp.float32).T

        top = jnp.full((8, rows), NEG, jnp.float32)
        for c in range(nclean // WIDE):
            s = lax.dot_general(chunk(ks, c), q, (((1,), (1,)), ((), ())), preferred_element_type=jnp.float32)
            for i in range(WIDE):
                part = s[i * BLK : (i + 1) * BLK] * SCALE2
                part = part + jnp.where(WIDE * c + i > index, NEG, 0.0).astype(jnp.float32)
                st[c, i * BLK : (i + 1) * BLK, :] = part
                top = jnp.maximum(top, jnp.max(part.reshape(BLK // 8, 8, rows), axis=0))
        top = jnp.max(top, axis=0, keepdims=True)
        total = jnp.zeros((8, rows), jnp.float32)
        acc = jnp.zeros((HEAD, rows), jnp.float32)
        for c in range(nclean // WIDE):
            e = jnp.exp2(st[c] - top)
            total = total + jnp.sum(e.reshape(wide // 8, 8, rows), axis=0)
            acc = acc + jnp.dot(chunk_t(vt, c), e.astype(jnp.bfloat16), preferred_element_type=jnp.float32)
        total = jnp.sum(total, axis=0, keepdims=True)
        attn_t = (acc / total).astype(jnp.bfloat16).astype(jnp.float32)
        delta = jnp.sum(do_t * attn_t, axis=0, keepdims=True)
        attn = attn_t.T.astype(jnp.bfloat16)
        for h in range(group):
            attn_ref[pl.ds(j * BLK, BLK), h * HEAD : (h + 1) * HEAD] = attn[h * BLK : (h + 1) * BLK]
        top = top + jnp.log2(total)
        acc = jnp.zeros((HEAD, rows), jnp.float32)
        for c in range(nclean // WIDE):
            p = jnp.exp2(st[c] - top)
            dp = lax.dot_general(chunk(vs, c), do, (((1,), (1,)), ((), ())), preferred_element_type=jnp.float32)
            ds = (p * (dp - delta)).astype(jnp.bfloat16)
            dvc = jnp.dot(p.astype(jnp.bfloat16), do, preferred_element_type=jnp.float32)
            dkc = jnp.dot(ds, q, preferred_element_type=jnp.float32)
            dv[pl.ds(nclean + WIDE * c, WIDE)] += dvc.reshape(WIDE, BLK, HEAD)
            dk[pl.ds(nclean + WIDE * c, WIDE)] += dkc.reshape(WIDE, BLK, HEAD)
            acc = acc + jnp.dot(chunk_t(kt, c), ds, preferred_element_type=jnp.float32)
        dq = (acc * SCALE).T
        for h in range(group):
            dq_ref[pl.ds(j * BLK, BLK), h * HEAD : (h + 1) * HEAD] = dq[h * BLK : (h + 1) * BLK]

        @pl.when(noisy)
        def _():
            for ref, ref_t, grad in ((ks, kt, dk), (vs, vt, dv)):
                ref[slot] = ref[spare]
                ref_t[pair] = ref_t[nclean // 2]
                grad[own] = grad[slot]
                grad[slot] = grad[spare]

        return unused

    lax.fori_loop(0, own_blocks, one_block, 0)
    for far in range(SIDE):
        for near in range(SIDE):
            base = place_of(far, near) * own_blocks
            for b in range(own_blocks):
                tag = tags_ref[base + b]
                part = slice((near * own_blocks + b) * BLK, (near * own_blocks + b + 1) * BLK)
                outs[far][part, 0:HEAD] = (dk[tag] * SCALE).astype(jnp.bfloat16)
                outs[far][part, HEAD:] = dv[tag].astype(jnp.bfloat16)


def attention(tags, q, do, pieces, g, group):
    tok = q.shape[0]
    nclean = tags.shape[0] // 2
    rows = group * BLK
    blocks = 2 * nclean + 1
    return pl.pallas_call(
        functools.partial(
            attention_kernel, first=g * group, nclean=nclean, own_blocks=tok // BLK, group=group
        ),
        in_specs=[SMEM] + [VMEM] * 6,
        out_specs=[VMEM] * 6,
        out_shape=[shape((tok, group * HEAD), jnp.bfloat16), shape((tok, group * HEAD), jnp.float32)]
        + [shape(pieces[0].shape, jnp.bfloat16)] * 4,
        scratch_shapes=[
            pltpu.VMEM((blocks, BLK, HEAD), jnp.bfloat16),
            pltpu.VMEM((blocks, BLK, HEAD), jnp.bfloat16),
            pltpu.VMEM((nclean // 2 + 1, HEAD, 2 * BLK), jnp.bfloat16),
            pltpu.VMEM((nclean // 2 + 1, HEAD, 2 * BLK), jnp.bfloat16),
            pltpu.VMEM((blocks, BLK, HEAD), jnp.float32),
            pltpu.VMEM((blocks, BLK, HEAD), jnp.float32),
            pltpu.VMEM((nclean // WIDE, WIDE * BLK, rows), jnp.float32),
        ],
        compiler_params=params(),
        cost_estimate=cost(6 << 30, 4 << 20),
        name="attention",
    )(tags, q, do, *pieces)


def query_back_kernel(q_ref, a_ref, b_ref, gain_ref, cos_ref, sin_ref, out_ref):
    gain, cosine, sine = gain_ref[...], cos_ref[...], sin_ref[...]
    heads = a_ref.shape[1] // HEAD
    for h in range(2 * heads):
        cols = slice(h * HEAD, (h + 1) * HEAD)
        source = (a_ref, b_ref)[h // heads]
        dy = source[:, (h % heads) * HEAD : (h % heads + 1) * HEAD]
        out_ref[:, cols] = norm_rope_back(q_ref[:, cols].astype(jnp.float32), dy, gain, cosine, sine)


def query_back(q_raw, dq0, dq1, gain, cosine, sine):
    return pl.pallas_call(
        query_back_kernel,
        grid=(1,),
        in_specs=[whole(*q_raw.shape), VMEM, VMEM, whole(*gain.shape), VMEM, VMEM],
        out_specs=whole(*q_raw.shape),
        out_shape=shape(q_raw.shape, jnp.float32),
        compiler_params=params(),
        cost_estimate=cost(0, 8 << 20),
        name="query_back",
    )(q_raw, dq0, dq1, gain, cosine, sine)


def key_back_kernel(key_ref, gain_ref, cos_ref, sin_ref, a, b, c, d, dk_ref, dv_ref):
    gain, cosine, sine = gain_ref[...], cos_ref[...], sin_ref[...]
    for g in range(a.shape[0]):
        cols = slice(g * HEAD, (g + 1) * HEAD)
        total = a[g].astype(jnp.float32) + b[g].astype(jnp.float32)
        total += c[g].astype(jnp.float32) + d[g].astype(jnp.float32)
        x = key_ref[:, cols].astype(jnp.float32)
        dk_ref[:, cols] = norm_rope_back(x, total[:, 0:HEAD], gain, cosine, sine)
        dv_ref[:, cols] = total[:, HEAD:]


def key_back(keys, gain, cosine, sine, parts):
    return pl.pallas_call(
        key_back_kernel,
        grid=(1,),
        in_specs=[whole(*keys.shape), whole(*gain.shape)] + [VMEM] * 6,
        out_specs=[whole(*keys.shape)] * 2,
        out_shape=[shape(keys.shape, jnp.float32)] * 2,
        compiler_params=params(),
        cost_estimate=cost(0, 2 << 20),
        name="key_back",
    )(keys, gain, cosine, sine, *parts)


def fold_kernel(*refs):
    parts, outs = refs[:-SIDE], refs[-SIDE:]
    rows = outs[0].shape[1]
    for g in range(len(parts) // SIDE):
        a, b, c, d = parts[SIDE * g : SIDE * g + SIDE]
        for i, out in enumerate(outs):
            part = slice(i * rows, (i + 1) * rows)
            total = a[part, :].astype(jnp.float32) + b[part, :].astype(jnp.float32)
            total += c[part, :].astype(jnp.float32) + d[part, :].astype(jnp.float32)
            out[g] = total.astype(jnp.bfloat16)


def fold(heads):
    rows, width = heads[0][0].shape
    return pl.pallas_call(
        fold_kernel,
        in_specs=[VMEM] * (SIDE * len(heads)),
        out_specs=[VMEM] * SIDE,
        out_shape=[shape((len(heads), rows // SIDE, width), jnp.bfloat16)] * SIDE,
        compiler_params=params(),
        cost_estimate=cost(0, 4 << 20),
        name="fold",
    )(*(part for parts in heads for part in parts))


def hop(value, steps, phase):
    pairs = []
    for y in range(SIDE):
        for x in range(SIDE):
            for f in range(4):
                dx, dy = (steps, 0) if (f + phase) % 2 == 0 else (0, steps)
                there = (y + dy) % SIDE * SIDE + (x + dx) % SIDE
                pairs.append(((y * SIDE + x) * 4 + f, there * 4 + f))
    return lax.ppermute(value, ("ctx", "ffn"), pairs)


def across(value, mask):
    return lax.ppermute(value, "ffn", [(s, s ^ mask) for s in range(4)])


def spread(value, phase):
    return [value] + [hop(value, k, phase) for k in range(1, SIDE)]


def collect(values, phase):
    return [values[0]] + [hop(values[k], -k, phase) for k in range(1, SIDE)]


def per_device(q_raw, keys, values, q_gain, k_gain, block_tags, w_out, d_out):
    nclean = block_tags.shape[0] // 2
    me = lax.axis_index("ffn").astype(jnp.int32)[None]
    heads = keys.shape[1] // HEAD
    group = q_raw.shape[1] // keys.shape[1]
    q_gain, k_gain = q_gain[None, :], k_gain[None, :]
    table = jnp.asarray(angle_table(nclean))

    kv, cosine, sine = key_prep(block_tags, keys, values, k_gain, table, heads)
    near = spread(kv, 0)
    far = across(d_out, 2)
    d_pieces = [d_out, across(d_out, 1), far, across(far, 1)]
    q = query_prep(q_raw, q_gain, cosine, sine)
    do = d_attn_product(me, d_pieces, w_out)

    pieces = []
    for g in range(heads):
        line = jnp.concatenate([part[g] for part in near], axis=0)
        if g:
            line, do, pieces[g - 1] = lax.optimization_barrier((line, do, pieces[g - 1]))
        pieces.append(spread(line, 1))

    attn, dq, sums = [], [], []
    for g in range(heads):
        results = attention(block_tags, q, do, pieces[g], g, group)
        if g:
            results, sums[g - 1] = lax.optimization_barrier((results, sums[g - 1]))
        attn_g, dq_g, *grads = results
        attn.append(attn_g)
        dq.append(dq_g)
        sums.append(collect(grads, 1))
    parts = collect(fold(sums), 0)

    send, keep = out_product(me, attn[0], attn[1], w_out)
    summed = keep.astype(jnp.float32) + across(send, 1).astype(jnp.float32)
    other = across(summed[1].astype(jnp.bfloat16), 2)
    attn_out = (summed[0] + other.astype(jnp.float32)).astype(jnp.bfloat16)
    d_q = query_back(q_raw, dq[0], dq[1], q_gain, cosine, sine)
    key_gradient, value_gradient = key_back(keys, k_gain, cosine, sine, parts)
    return attn_out, d_q, key_gradient, value_gradient


def solution(mesh):
    split = P(("dp", "ctx"), "ffn")
    return jax.shard_map(
        per_device,
        mesh=mesh,
        in_specs=(split, split, split, P(), P(), P("dp"), P("ffn", None), split),
        out_specs=(split,) * 4,
        check_vma=False,
    )
```

```python
import functools

import jax
import jax.numpy as jnp
import numpy as np
from jax import lax
from jax.experimental import pallas as pl
from jax.experimental.pallas import tpu as pltpu
from jax.sharding import PartitionSpec as P

HEAD = 128
BLK = 64
ROPE_BASE = 1000000.0
EPS = 1e-06
NEG = -1e30
SCALE = HEAD ** (-0.5)
SCALE2 = SCALE * 1.4426950408889634
WIDE = 8
SIDE = 4
VMEM = pl.BlockSpec(memory_space=pltpu.VMEM)
SMEM = pl.BlockSpec(memory_space=pltpu.SMEM)
HBM = pl.BlockSpec(memory_space=pltpu.HBM)
LIMIT = 32 * 1024 * 1024


def shape(dims, dtype):
    return jax.ShapeDtypeStruct(dims, dtype)


def params(limit=LIMIT):
    return pltpu.CompilerParams(vmem_limit_bytes=limit)


def cost(flops, nbytes):
    return pl.CostEstimate(flops=flops, bytes_accessed=nbytes, transcendentals=0)


def angle_table(blocks):
    freq = ROPE_BASE ** (-(np.arange(HEAD // 2) * 2.0 / HEAD))
    freq = np.concatenate([freq, freq])[None, :]
    inner = np.arange(BLK)[:, None] * freq
    outer = (np.arange(blocks) * BLK)[:, None] * freq
    return np.concatenate([np.cos(inner), np.sin(inner), np.cos(outer), np.sin(outer)]).astype(np.float32)


def half_sign():
    lane = lax.broadcasted_iota(jnp.int32, (1, HEAD), 1)
    return jnp.where(lane < HEAD // 2, -1.0, 1.0).astype(jnp.float32)


def block_angles(table_ref, index, blocks):
    c_in, s_in = table_ref[0:BLK, :], table_ref[BLK : 2 * BLK, :]
    c_out = table_ref[pl.ds(2 * BLK + index, 1), :]
    s_out = table_ref[pl.ds(2 * BLK + blocks + index, 1), :]
    return c_in * c_out - s_in * s_out, s_in * c_out + c_in * s_out


def norm_rope(x, gain, cosine, sine_signed):
    normed = x * lax.rsqrt(jnp.mean(x * x, axis=-1, keepdims=True) + EPS) * gain
    return normed * cosine + pltpu.roll(normed, HEAD // 2, 1) * sine_signed


def norm_rope_back(x, dy, gain, cosine, sine_signed):
    inv = lax.rsqrt(jnp.mean(x * x, axis=-1, keepdims=True) + EPS)
    dn = (dy * cosine + pltpu.roll(dy * sine_signed, HEAD // 2, 1)) * gain
    inner = jnp.mean(x * dn, axis=-1, keepdims=True)
    return inv * dn - x * (inv * inv * inv * inner)


def whole(*dims):
    return pl.BlockSpec(dims, lambda i: (0,) * len(dims))


def key_kernel(
    tags_ref, key_hbm, value_hbm, gain_hbm, table_hbm, out_ref, cos_ref, sin_ref, key_ref, gain_ref, table_ref, sems, *, blocks
):
    heads, tok = out_ref.shape[0], key_ref.shape[0]
    copies = [
        pltpu.make_async_copy(source, dest, sems.at[i])
        for i, (source, dest) in enumerate(((key_hbm, key_ref), (gain_hbm, gain_ref), (table_hbm, table_ref)))
    ]
    copies += [
        pltpu.make_async_copy(value_hbm.at[:, pl.ds(g * HEAD, HEAD)], out_ref.at[g, :, pl.ds(HEAD, HEAD)], sems.at[3 + g])
        for g in range(heads)
    ]
    for copy in copies:
        copy.start()
    for copy in copies[:3]:
        copy.wait()
    gain, sign = gain_ref[...], half_sign()
    own_blocks = tok // BLK
    base = place_of(0, 0) * own_blocks
    for j in range(own_blocks):
        rows = slice(j * BLK, (j + 1) * BLK)
        cosine, sine = block_angles(table_ref, tags_ref[base + j] % blocks, blocks)
        sine = sine * sign
        cos_ref[rows, :] = cosine
        sin_ref[rows, :] = sine
        for g in range(heads):
            x = key_ref[rows, g * HEAD : (g + 1) * HEAD].astype(jnp.float32)
            out_ref[g, rows, 0:HEAD] = norm_rope(x, gain, cosine, sine).astype(jnp.bfloat16)
    for copy in copies[3:]:
        copy.wait()


def key_prep(tags, keys, values, gain, table, heads):
    tok = keys.shape[0]
    blocks = (table.shape[0] - 2 * BLK) // 2
    return pl.pallas_call(
        functools.partial(key_kernel, blocks=blocks),
        in_specs=[SMEM] + [HBM] * 4,
        out_specs=[VMEM] * 3,
        out_shape=[shape((heads, tok, 2 * HEAD), jnp.bfloat16)] + [shape((tok, HEAD), jnp.float32)] * 2,
        scratch_shapes=[
            pltpu.VMEM(keys.shape, keys.dtype),
            pltpu.VMEM(gain.shape, gain.dtype),
            pltpu.VMEM(table.shape, table.dtype),
            pltpu.SemaphoreType.DMA((3 + heads,)),
        ],
        compiler_params=params(63 * 1024 * 1024),
        cost_estimate=cost(0, 1 << 20),
        name="key_prep",
    )(tags, keys, values, gain, table)


def query_kernel(q_ref, gain_ref, cos_ref, sin_ref, out_ref):
    gain, cosine, sine = gain_ref[...], cos_ref[...], sin_ref[...]
    for h in range(q_ref.shape[1] // HEAD):
        cols = slice(h * HEAD, (h + 1) * HEAD)
        x = q_ref[:, cols].astype(jnp.float32)
        out_ref[:, cols] = norm_rope(x, gain, cosine, sine).astype(jnp.bfloat16)


def query_prep(q_raw, gain, cosine, sine):
    return pl.pallas_call(
        query_kernel,
        grid=(1,),
        in_specs=[whole(*q_raw.shape), whole(*gain.shape), whole(*cosine.shape), whole(*sine.shape)],
        out_specs=whole(*q_raw.shape),
        out_shape=shape(q_raw.shape, jnp.bfloat16),
        compiler_params=params(63 * 1024 * 1024),
        cost_estimate=cost(0, 4 << 20),
        name="query_prep",
    )(q_raw, gain, cosine, sine)


def d_attn_kernel(me_ref, p0, p1, p2, p3a, p3b, w_ref, out_ref, acc):
    k = pl.program_id(0)

    def product(piece):
        return lax.dot_general(piece[...], w_ref[...], (((1,), (1,)), ((), ())), preferred_element_type=jnp.float32)

    @pl.when(k == 0)
    def _():
        acc[...] = product(p0)

    @pl.when(k == 1)
    def _():
        acc[...] += product(p1)

    @pl.when(k == 2)
    def _():
        acc[...] += product(p2)

    @pl.when(k == 3)
    def _():
        rows = p3a.shape[0]
        out_ref[:rows] = (acc[:rows] + product(p3a)).astype(jnp.bfloat16)
        out_ref[rows:] = (acc[rows:] + product(p3b)).astype(jnp.bfloat16)


def d_attn_product(me, pieces, w_out):
    tok, width = pieces[0].shape
    feats = w_out.shape[0]
    place = lambda k, me: (0, 0)
    return pl.pallas_call(
        d_attn_kernel,
        grid_spec=pltpu.PrefetchScalarGridSpec(
            num_scalar_prefetch=1,
            grid=(4,),
            in_specs=[pl.BlockSpec(piece.shape, place) for piece in pieces]
            + [pl.BlockSpec((feats, width), lambda k, me: (0, me[0] ^ k))],
            out_specs=pl.BlockSpec((tok, feats), place),
            scratch_shapes=[pltpu.VMEM((tok, feats), jnp.float32)],
        ),
        out_shape=shape((tok, feats), jnp.bfloat16),
        compiler_params=params(),
        cost_estimate=cost(1, 1),
        name="d_attn_product",
    )(me, *pieces, w_out)


def out_kernel(me_ref, a0_ref, a1_ref, w_ref, far_a, far_b, keep_far, near, keep_near):
    k = pl.program_id(0)
    half = a0_ref.shape[1]
    term = jnp.dot(a0_ref[...], w_ref[0:half, :], preferred_element_type=jnp.float32)
    term += jnp.dot(a1_ref[...], w_ref[half:, :], preferred_element_type=jnp.float32)
    term = term.astype(jnp.bfloat16)
    rows = far_a.shape[0]

    @pl.when(k == 0)
    def _():
        far_a[...] = term[:rows]
        far_b[...] = term[rows:]

    for i, out in enumerate((keep_far, near, keep_near)):

        @pl.when(k == i + 1)
        def _(out=out):
            out[...] = term


def out_product(me, a0, a1, w_out):
    tok = a0.shape[0]
    feats, wide = w_out.shape
    width = wide // 4
    place = lambda k, me: (0, 0)
    dims = [(tok // 2, width)] * 2 + [(tok, width)] * 3
    return pl.pallas_call(
        out_kernel,
        grid_spec=pltpu.PrefetchScalarGridSpec(
            num_scalar_prefetch=1,
            grid=(4,),
            in_specs=[pl.BlockSpec(a0.shape, place)] * 2
            + [pl.BlockSpec((feats, width), lambda k, me: (0, me[0] ^ (3 - k)))],
            out_specs=[pl.BlockSpec(d, place) for d in dims],
        ),
        out_shape=[shape(d, jnp.bfloat16) for d in dims],
        compiler_params=params(),
        cost_estimate=cost(1, 1),
        name="out_product",
    )(me, a0, a1, w_out)


def place_of(far, near):
    here = lax.axis_index("ctx")
    first = lax.axis_index("ffn") % 2 == 0
    dx = jnp.where(first, near, far)
    dy = jnp.where(first, far, near)
    return (here // SIDE - dy + SIDE) % SIDE * SIDE + (here % SIDE - dx + SIDE) % SIDE


def attention_kernel(tags_ref, q_ref, do_ref, *refs, first, nclean, own_blocks, group):
    pieces, (attn_ref, dq_ref), outs = refs[0:4], refs[4:6], refs[6:10]
    ks, vs, kt, vt, dk, dv, st = refs[10:]
    spare = 2 * nclean
    rows = group * BLK
    wide = WIDE * BLK
    own_base = place_of(0, 0) * own_blocks
    for far in range(SIDE):
        for near in range(SIDE):
            base = place_of(far, near) * own_blocks
            for b in range(own_blocks):
                tag = tags_ref[base + b]
                part = slice((near * own_blocks + b) * BLK, (near * own_blocks + b + 1) * BLK)
                ks[tag] = pieces[far][part, 0:HEAD]
                vs[tag] = pieces[far][part, HEAD:]

    def flip(ref, pair):
        return ref[pl.ds(nclean + 2 * pair, 2)].reshape(2 * BLK, HEAD).astype(jnp.float32).T.astype(jnp.bfloat16)

    def chunk(ref, c):
        return ref[pl.ds(nclean + WIDE * c, WIDE)].reshape(wide, HEAD)

    def chunk_t(ref, c):
        return jnp.concatenate([ref[WIDE // 2 * c + i] for i in range(WIDE // 2)], axis=1)

    for pair in range(nclean // 2):
        kt[pair] = flip(ks, pair)
        vt[pair] = flip(vs, pair)
    dk[...] = jnp.zeros_like(dk)
    dv[...] = jnp.zeros_like(dv)

    def gather(ref, j):
        return jnp.concatenate(
            [ref[pl.ds(j * BLK, BLK), (first + h) * HEAD : (first + h + 1) * HEAD] for h in range(group)], axis=0
        )

    def one_block(j, unused):
        own = tags_ref[own_base + j]
        noisy = own < nclean
        index = own % nclean
        slot = nclean + index
        pair = index // 2

        @pl.when(noisy)
        def _():
            for ref, ref_t, grad in ((ks, kt, dk), (vs, vt, dv)):
                ref[spare] = ref[slot]
                ref[slot] = ref[own]
                ref_t[nclean // 2] = ref_t[pair]
                ref_t[pair] = flip(ref, pair)
                grad[spare] = grad[slot]
                grad[slot] = jnp.zeros((BLK, HEAD), jnp.float32)

        q = gather(q_ref, j)
        do = gather(do_ref, j)
        do_t = do.astype(jnp.float32).T

        for c in range(nclean // WIDE):
            st[c] = lax.dot_general(chunk(ks, c), q, (((1,), (1,)), ((), ())), preferred_element_type=jnp.float32)
        hidden = [jnp.where(i > index, NEG, 0.0).astype(jnp.float32) for i in range(nclean)]
        top = jnp.full((8, rows), NEG, jnp.float32)
        for c in range(nclean // WIDE):
            for i in range(WIDE):
                part = jnp.max(st[c, i * BLK : (i + 1) * BLK, :].reshape(BLK // 8, 8, rows), axis=0)
                top = jnp.maximum(top, part + hidden[WIDE * c + i])
        top = jnp.max(top, axis=0, keepdims=True) * SCALE2

        def weight(c, shift):
            return jnp.concatenate(
                [
                    jnp.exp2(st[c, i * BLK : (i + 1) * BLK, :] * SCALE2 + (hidden[WIDE * c + i] - shift))
                    for i in range(WIDE)
                ],
                axis=0,
            )

        total = jnp.zeros((8, rows), jnp.float32)
        acc = jnp.zeros((HEAD, rows), jnp.float32)
        for c in range(nclean // WIDE):
            e = weight(c, top)
            total = total + jnp.sum(e.reshape(wide // 8, 8, rows), axis=0)
            acc = acc + jnp.dot(chunk_t(vt, c), e.astype(jnp.bfloat16), preferred_element_type=jnp.float32)
        total = jnp.sum(total, axis=0, keepdims=True)
        attn_t = (acc / total).astype(jnp.bfloat16).astype(jnp.float32)
        delta = jnp.sum(do_t * attn_t, axis=0, keepdims=True)
        attn = attn_t.T.astype(jnp.bfloat16)
        for h in range(group):
            attn_ref[pl.ds(j * BLK, BLK), h * HEAD : (h + 1) * HEAD] = attn[h * BLK : (h + 1) * BLK]
        top = top + jnp.log2(total)
        acc = jnp.zeros((HEAD, rows), jnp.float32)
        for c in range(nclean // WIDE):
            p = weight(c, top)
            dp = lax.dot_general(chunk(vs, c), do, (((1,), (1,)), ((), ())), preferred_element_type=jnp.float32)
            ds = (p * (dp - delta)).astype(jnp.bfloat16)
            dvc = jnp.dot(p.astype(jnp.bfloat16), do, preferred_element_type=jnp.float32)
            dkc = jnp.dot(ds, q, preferred_element_type=jnp.float32)
            dv[pl.ds(nclean + WIDE * c, WIDE)] += dvc.reshape(WIDE, BLK, HEAD)
            dk[pl.ds(nclean + WIDE * c, WIDE)] += dkc.reshape(WIDE, BLK, HEAD)
            acc = acc + jnp.dot(chunk_t(kt, c), ds, preferred_element_type=jnp.float32)
        dq = (acc * SCALE).T
        for h in range(group):
            dq_ref[pl.ds(j * BLK, BLK), h * HEAD : (h + 1) * HEAD] = dq[h * BLK : (h + 1) * BLK]

        @pl.when(noisy)
        def _():
            for ref, ref_t, grad in ((ks, kt, dk), (vs, vt, dv)):
                ref[slot] = ref[spare]
                ref_t[pair] = ref_t[nclean // 2]
                grad[own] = grad[slot]
                grad[slot] = grad[spare]

        return unused

    lax.fori_loop(0, own_blocks, one_block, 0)
    for far in range(SIDE):
        for near in range(SIDE):
            base = place_of(far, near) * own_blocks
            for b in range(own_blocks):
                tag = tags_ref[base + b]
                part = slice((near * own_blocks + b) * BLK, (near * own_blocks + b + 1) * BLK)
                outs[far][part, 0:HEAD] = (dk[tag] * SCALE).astype(jnp.bfloat16)
                outs[far][part, HEAD:] = dv[tag].astype(jnp.bfloat16)


def attention(tags, q, do, pieces, g, group):
    tok = q.shape[0]
    nclean = tags.shape[0] // 2
    rows = group * BLK
    blocks = 2 * nclean + 1
    return pl.pallas_call(
        functools.partial(
            attention_kernel, first=g * group, nclean=nclean, own_blocks=tok // BLK, group=group
        ),
        in_specs=[SMEM] + [VMEM] * 6,
        out_specs=[VMEM] * 6,
        out_shape=[shape((tok, group * HEAD), jnp.bfloat16), shape((tok, group * HEAD), jnp.float32)]
        + [shape(pieces[0].shape, jnp.bfloat16)] * 4,
        scratch_shapes=[
            pltpu.VMEM((blocks, BLK, HEAD), jnp.bfloat16),
            pltpu.VMEM((blocks, BLK, HEAD), jnp.bfloat16),
            pltpu.VMEM((nclean // 2 + 1, HEAD, 2 * BLK), jnp.bfloat16),
            pltpu.VMEM((nclean // 2 + 1, HEAD, 2 * BLK), jnp.bfloat16),
            pltpu.VMEM((blocks, BLK, HEAD), jnp.float32),
            pltpu.VMEM((blocks, BLK, HEAD), jnp.float32),
            pltpu.VMEM((nclean // WIDE, WIDE * BLK, rows), jnp.float32),
        ],
        compiler_params=params(),
        cost_estimate=cost(6 << 30, 4 << 20),
        name="attention",
    )(tags, q, do, *pieces)


def query_back_kernel(q_ref, a_ref, b_ref, gain_ref, cos_ref, sin_ref, out_ref):
    gain, cosine, sine = gain_ref[...], cos_ref[...], sin_ref[...]
    heads = a_ref.shape[1] // HEAD
    for h in range(2 * heads):
        cols = slice(h * HEAD, (h + 1) * HEAD)
        source = (a_ref, b_ref)[h // heads]
        dy = source[:, (h % heads) * HEAD : (h % heads + 1) * HEAD]
        out_ref[:, cols] = norm_rope_back(q_ref[:, cols].astype(jnp.float32), dy, gain, cosine, sine)


def query_back(q_raw, dq0, dq1, gain, cosine, sine):
    return pl.pallas_call(
        query_back_kernel,
        grid=(1,),
        in_specs=[whole(*q_raw.shape), VMEM, VMEM, whole(*gain.shape), VMEM, VMEM],
        out_specs=whole(*q_raw.shape),
        out_shape=shape(q_raw.shape, jnp.float32),
        compiler_params=params(),
        cost_estimate=cost(1, 1),
        name="query_back",
    )(q_raw, dq0, dq1, gain, cosine, sine)


def finish_kernel(key_ref, gain_ref, cos_ref, sin_ref, a, b, c, d, keep, near, far, out_ref, dk_ref, dv_ref):
    out = keep[...].astype(jnp.float32) + near[...].astype(jnp.float32) + far[...].astype(jnp.float32)
    out_ref[...] = out.astype(jnp.bfloat16)
    gain, cosine, sine = gain_ref[...], cos_ref[...], sin_ref[...]
    for g in range(a.shape[0]):
        cols = slice(g * HEAD, (g + 1) * HEAD)
        total = a[g].astype(jnp.float32) + b[g].astype(jnp.float32)
        total += c[g].astype(jnp.float32) + d[g].astype(jnp.float32)
        x = key_ref[:, cols].astype(jnp.float32)
        dk_ref[:, cols] = norm_rope_back(x, total[:, 0:HEAD], gain, cosine, sine)
        dv_ref[:, cols] = total[:, HEAD:]


def finish(keys, gain, cosine, sine, parts, terms):
    return pl.pallas_call(
        finish_kernel,
        grid=(1,),
        in_specs=[whole(*keys.shape), whole(*gain.shape)] + [VMEM] * 9,
        out_specs=[whole(*terms[0].shape)] + [whole(*keys.shape)] * 2,
        out_shape=[shape(terms[0].shape, jnp.bfloat16)] + [shape(keys.shape, jnp.float32)] * 2,
        compiler_params=params(),
        cost_estimate=cost(0, 2 << 20),
        name="finish",
    )(keys, gain, cosine, sine, *parts, *terms)


def fold_kernel(*refs):
    parts, outs = refs[:-SIDE], refs[-SIDE:]
    rows = outs[0].shape[1]
    for g in range(len(parts) // SIDE):
        a, b, c, d = parts[SIDE * g : SIDE * g + SIDE]
        for i, out in enumerate(outs):
            part = slice(i * rows, (i + 1) * rows)
            total = a[part, :].astype(jnp.float32) + b[part, :].astype(jnp.float32)
            total += c[part, :].astype(jnp.float32) + d[part, :].astype(jnp.float32)
            out[g] = total.astype(jnp.bfloat16)


def fold(heads):
    rows, width = heads[0][0].shape
    return pl.pallas_call(
        fold_kernel,
        in_specs=[VMEM] * (SIDE * len(heads)),
        out_specs=[VMEM] * SIDE,
        out_shape=[shape((len(heads), rows // SIDE, width), jnp.bfloat16)] * SIDE,
        compiler_params=params(),
        cost_estimate=cost(0, 4 << 20),
        name="fold",
    )(*(part for parts in heads for part in parts))


def hop(value, steps, phase):
    pairs = []
    for y in range(SIDE):
        for x in range(SIDE):
            for f in range(4):
                dx, dy = (steps, 0) if (f + phase) % 2 == 0 else (0, steps)
                there = (y + dy) % SIDE * SIDE + (x + dx) % SIDE
                pairs.append(((y * SIDE + x) * 4 + f, there * 4 + f))
    return lax.ppermute(value, ("ctx", "ffn"), pairs)


def across(value, mask):
    return lax.ppermute(value, "ffn", [(s, s ^ mask) for s in range(4)])


def spread(value, phase):
    return [value] + [hop(value, k, phase) for k in range(1, SIDE)]


def collect(values, phase):
    return [values[0]] + [hop(values[k], -k, phase) for k in range(1, SIDE)]


def per_device(q_raw, keys, values, q_gain, k_gain, block_tags, w_out, d_out):
    nclean = block_tags.shape[0] // 2
    me = lax.axis_index("ffn").astype(jnp.int32)[None]
    heads = keys.shape[1] // HEAD
    group = q_raw.shape[1] // keys.shape[1]
    q_gain, k_gain = q_gain[None, :], k_gain[None, :]
    table = jnp.asarray(angle_table(nclean))

    kv, cosine, sine = key_prep(block_tags, keys, values, k_gain, table, heads)
    near = spread(kv, 0)
    q = query_prep(q_raw, q_gain, cosine, sine)
    lines = [jnp.concatenate([part[g] for part in near], axis=0) for g in range(heads)]
    lines[0], q = lax.optimization_barrier((lines[0], q))
    far = across(d_out, 2)
    half = far.shape[0] // 2
    d_pieces = [d_out, across(d_out, 1), far, across(far[:half], 1), across(far[half:], 1)]
    do = d_attn_product(me, d_pieces, w_out)

    pieces = []
    for g in range(heads):
        line = lines[g]
        if g:
            line, do, pieces[g - 1] = lax.optimization_barrier((line, do, pieces[g - 1]))
        pieces.append(spread(line, 1))

    attn, dq, sums = [], [], []
    for g in range(heads):
        results = attention(block_tags, q, do, pieces[g], g, group)
        if g:
            results, sums[g - 1] = lax.optimization_barrier((results, sums[g - 1]))
        attn_g, dq_g, *grads = results
        attn.append(attn_g)
        dq.append(dq_g)
        sums.append(collect(grads, 1))
    far_a, far_b, keep_far, near, keep_near = out_product(me, attn[0], attn[1], w_out)
    far = jnp.concatenate([across(far_a, 1), across(far_b, 1)], axis=0)
    far = (keep_far.astype(jnp.float32) + far.astype(jnp.float32)).astype(jnp.bfloat16)
    shares, far, near = lax.optimization_barrier((fold(sums), far, near))
    parts = collect(shares, 0)
    terms = [keep_near, across(near, 1), across(far, 2)]
    d_q = query_back(q_raw, dq[0], dq[1], q_gain, cosine, sine)
    attn_out, key_gradient, value_gradient = finish(keys, k_gain, cosine, sine, parts, terms)
    return attn_out, d_q, key_gradient, value_gradient


def solution(mesh):
    split = P(("dp", "ctx"), "ffn")
    return jax.shard_map(
        per_device,
        mesh=mesh,
        in_specs=(split, split, split, P(), P(), P("dp"), P("ffn", None), split),
        out_specs=(split,) * 4,
        check_vma=False,
    )
```

```python
import functools

import jax
import jax.numpy as jnp
import numpy as np
from jax import lax
from jax.experimental import pallas as pl
from jax.experimental.pallas import tpu as pltpu
from jax.sharding import PartitionSpec as P

HEAD = 128
BLK = 64
ROPE_BASE = 1000000.0
EPS = 1e-06
NEG = -1e30
SCALE = HEAD ** (-0.5)
SCALE2 = SCALE * 1.4426950408889634
WIDE = 8
SCORE_WIDE = 4
WEIGH_WIDE = 16
SIDE = 4
VMEM = pl.BlockSpec(memory_space=pltpu.VMEM)
SMEM = pl.BlockSpec(memory_space=pltpu.SMEM)
HBM = pl.BlockSpec(memory_space=pltpu.HBM)
LIMIT = 32 * 1024 * 1024


def shape(dims, dtype):
    return jax.ShapeDtypeStruct(dims, dtype)


def params(limit=LIMIT):
    return pltpu.CompilerParams(vmem_limit_bytes=limit)


def cost(flops, nbytes):
    return pl.CostEstimate(flops=flops, bytes_accessed=nbytes, transcendentals=0)


def angle_table(blocks):
    freq = ROPE_BASE ** (-(np.arange(HEAD // 2) * 2.0 / HEAD))
    freq = np.concatenate([freq, freq])[None, :]
    inner = np.arange(BLK)[:, None] * freq
    outer = (np.arange(blocks) * BLK)[:, None] * freq
    return np.concatenate([np.cos(inner), np.sin(inner), np.cos(outer), np.sin(outer)]).astype(np.float32)


def half_sign():
    lane = lax.broadcasted_iota(jnp.int32, (1, HEAD), 1)
    return jnp.where(lane < HEAD // 2, -1.0, 1.0).astype(jnp.float32)


def block_angles(table_ref, index, blocks):
    c_in, s_in = table_ref[0:BLK, :], table_ref[BLK : 2 * BLK, :]
    c_out = table_ref[pl.ds(2 * BLK + index, 1), :]
    s_out = table_ref[pl.ds(2 * BLK + blocks + index, 1), :]
    return c_in * c_out - s_in * s_out, s_in * c_out + c_in * s_out


def norm_rope(x, gain, cosine, sine_signed):
    normed = x * lax.rsqrt(jnp.mean(x * x, axis=-1, keepdims=True) + EPS) * gain
    return normed * cosine + pltpu.roll(normed, HEAD // 2, 1) * sine_signed


def norm_rope_back(x, dy, gain, cosine, sine_signed):
    inv = lax.rsqrt(jnp.mean(x * x, axis=-1, keepdims=True) + EPS)
    dn = (dy * cosine + pltpu.roll(dy * sine_signed, HEAD // 2, 1)) * gain
    inner = jnp.mean(x * dn, axis=-1, keepdims=True)
    return inv * dn - x * (inv * inv * inv * inner)


def whole(*dims):
    return pl.BlockSpec(dims, lambda i: (0,) * len(dims))


def key_kernel(
    tags_ref, key_hbm, value_hbm, gain_hbm, table_hbm, out_ref, cos_ref, sin_ref, key_ref, gain_ref, table_ref, sems, *, blocks
):
    heads, tok = out_ref.shape[0], key_ref.shape[0]
    copies = [
        pltpu.make_async_copy(source, dest, sems.at[i])
        for i, (source, dest) in enumerate(((key_hbm, key_ref), (gain_hbm, gain_ref), (table_hbm, table_ref)))
    ]
    copies += [
        pltpu.make_async_copy(value_hbm.at[:, pl.ds(g * HEAD, HEAD)], out_ref.at[g, :, pl.ds(HEAD, HEAD)], sems.at[3 + g])
        for g in range(heads)
    ]
    for copy in copies:
        copy.start()
    for copy in copies[:3]:
        copy.wait()
    gain, sign = gain_ref[...], half_sign()
    own_blocks = tok // BLK
    base = place_of(0, 0) * own_blocks
    for j in range(own_blocks):
        rows = slice(j * BLK, (j + 1) * BLK)
        cosine, sine = block_angles(table_ref, tags_ref[base + j] % blocks, blocks)
        sine = sine * sign
        cos_ref[rows, :] = cosine
        sin_ref[rows, :] = sine
        for g in range(heads):
            x = key_ref[rows, g * HEAD : (g + 1) * HEAD].astype(jnp.float32)
            out_ref[g, rows, 0:HEAD] = norm_rope(x, gain, cosine, sine).astype(jnp.bfloat16)
    for copy in copies[3:]:
        copy.wait()


def key_prep(tags, keys, values, gain, table, heads):
    tok = keys.shape[0]
    blocks = (table.shape[0] - 2 * BLK) // 2
    return pl.pallas_call(
        functools.partial(key_kernel, blocks=blocks),
        in_specs=[SMEM] + [HBM] * 4,
        out_specs=[VMEM] * 3,
        out_shape=[shape((heads, tok, 2 * HEAD), jnp.bfloat16)] + [shape((tok, HEAD), jnp.float32)] * 2,
        scratch_shapes=[
            pltpu.VMEM(keys.shape, keys.dtype),
            pltpu.VMEM(gain.shape, gain.dtype),
            pltpu.VMEM(table.shape, table.dtype),
            pltpu.SemaphoreType.DMA((3 + heads,)),
        ],
        compiler_params=params(63 * 1024 * 1024),
        cost_estimate=cost(0, 1 << 20),
        name="key_prep",
    )(tags, keys, values, gain, table)


def query_kernel(q_ref, gain_ref, cos_ref, sin_ref, out_ref):
    gain, cosine, sine = gain_ref[...], cos_ref[...], sin_ref[...]
    for h in range(q_ref.shape[1] // HEAD):
        cols = slice(h * HEAD, (h + 1) * HEAD)
        x = q_ref[:, cols].astype(jnp.float32)
        out_ref[:, cols] = norm_rope(x, gain, cosine, sine).astype(jnp.bfloat16)


def query_prep(q_raw, gain, cosine, sine):
    return pl.pallas_call(
        query_kernel,
        grid=(1,),
        in_specs=[whole(*q_raw.shape), whole(*gain.shape), whole(*cosine.shape), whole(*sine.shape)],
        out_specs=whole(*q_raw.shape),
        out_shape=shape(q_raw.shape, jnp.bfloat16),
        compiler_params=params(63 * 1024 * 1024),
        cost_estimate=cost(0, 4 << 20),
        name="query_prep",
    )(q_raw, gain, cosine, sine)


def d_attn_kernel(me_ref, p0, p1, p2, p3a, p3b, w_ref, out_ref, acc):
    k = pl.program_id(0)

    def product(piece):
        return lax.dot_general(piece, w_ref[...], (((1,), (1,)), ((), ())), preferred_element_type=jnp.float32)

    @pl.when(k == 0)
    def _():
        acc[...] = product(p0[...])

    @pl.when(k == 1)
    def _():
        acc[...] += product(p1[...])

    @pl.when(k == 2)
    def _():
        acc[...] += product(p2[...])

    @pl.when(k == 3)
    def _():
        both = jnp.concatenate([p3a[...], p3b[...]], axis=0)
        out_ref[...] = (acc[...] + product(both)).astype(jnp.bfloat16)


def d_attn_product(me, pieces, w_out):
    tok, width = pieces[0].shape
    feats = w_out.shape[0]
    place = lambda k, me: (0, 0)
    return pl.pallas_call(
        d_attn_kernel,
        grid_spec=pltpu.PrefetchScalarGridSpec(
            num_scalar_prefetch=1,
            grid=(4,),
            in_specs=[pl.BlockSpec(piece.shape, place) for piece in pieces]
            + [pl.BlockSpec((feats, width), lambda k, me: (0, me[0] ^ k))],
            out_specs=pl.BlockSpec((tok, feats), place),
            scratch_shapes=[pltpu.VMEM((tok, feats), jnp.float32)],
        ),
        out_shape=shape((tok, feats), jnp.bfloat16),
        compiler_params=params(),
        cost_estimate=cost(1, 1),
        name="d_attn_product",
    )(me, *pieces, w_out)


def out_kernel(me_ref, a0_ref, a1_ref, w_ref, far_a, far_b, keep_far, near, keep_near):
    k = pl.program_id(0)
    half = a0_ref.shape[1]
    term = jnp.dot(a0_ref[...], w_ref[0:half, :], preferred_element_type=jnp.float32)
    term += jnp.dot(a1_ref[...], w_ref[half:, :], preferred_element_type=jnp.float32)
    term = term.astype(jnp.bfloat16)
    rows = far_a.shape[0]

    @pl.when(k == 0)
    def _():
        far_a[...] = term[:rows]
        far_b[...] = term[rows:]

    for i, out in enumerate((keep_far, near, keep_near)):

        @pl.when(k == i + 1)
        def _(out=out):
            out[...] = term


def out_product(me, a0, a1, w_out):
    tok = a0.shape[0]
    feats, wide = w_out.shape
    width = wide // 4
    place = lambda k, me: (0, 0)
    dims = [(tok // 2, width)] * 2 + [(tok, width)] * 3
    return pl.pallas_call(
        out_kernel,
        grid_spec=pltpu.PrefetchScalarGridSpec(
            num_scalar_prefetch=1,
            grid=(4,),
            in_specs=[pl.BlockSpec(a0.shape, place)] * 2
            + [pl.BlockSpec((feats, width), lambda k, me: (0, me[0] ^ (3 - k)))],
            out_specs=[pl.BlockSpec(d, place) for d in dims],
        ),
        out_shape=[shape(d, jnp.bfloat16) for d in dims],
        compiler_params=params(),
        cost_estimate=cost(1, 1),
        name="out_product",
    )(me, a0, a1, w_out)


def place_of(far, near):
    here = lax.axis_index("ctx")
    first = lax.axis_index("ffn") % 2 == 0
    dx = jnp.where(first, near, far)
    dy = jnp.where(first, far, near)
    return (here // SIDE - dy + SIDE) % SIDE * SIDE + (here % SIDE - dx + SIDE) % SIDE


def attention_kernel(tags_ref, q_ref, do_ref, *refs, first, nclean, own_blocks, group):
    pieces, (attn_ref, dq_ref), outs = refs[0:4], refs[4:6], refs[6:10]
    ks, vs, kt, vt, dk, dv, dk_own, dv_own, st = refs[10:]
    rows = group * BLK
    own_base = place_of(0, 0) * own_blocks
    for far in range(SIDE):
        for near in range(SIDE):
            base = place_of(far, near) * own_blocks
            for b in range(own_blocks):
                tag = tags_ref[base + b]
                part = slice((near * own_blocks + b) * BLK, (near * own_blocks + b + 1) * BLK)
                ks[tag] = pieces[far][part, 0:HEAD]
                vs[tag] = pieces[far][part, HEAD:]

    def flip(ref, pair):
        return ref[pl.ds(nclean + 2 * pair, 2)].reshape(2 * BLK, HEAD).astype(jnp.float32).T.astype(jnp.bfloat16)

    def blocks_of(ref, c, many):
        return ref[pl.ds(nclean + many * c, many)].reshape(many * BLK, HEAD)

    def chunk_t(ref, c, many):
        return jnp.concatenate([ref[many // 2 * c + i] for i in range(many // 2)], axis=1)

    for pair in range(nclean // 2):
        kt[pair] = flip(ks, pair)
        vt[pair] = flip(vs, pair)
    for grad in (dk, dv):
        grad[pl.ds(nclean, nclean)] = jnp.zeros((nclean, BLK, HEAD), jnp.float32)

    def gather(ref, j):
        return jnp.concatenate(
            [ref[j * BLK : (j + 1) * BLK, (first + h) * HEAD : (first + h + 1) * HEAD] for h in range(group)], axis=0
        )

    def weight(score, bias):
        return jnp.exp2(score * SCALE2 + bias)

    def nt(left, right):
        return lax.dot_general(left, right, (((1,), (1,)), ((), ())), preferred_element_type=jnp.float32)

    def tn(left, right):
        return lax.dot_general(left, right, (((0,), (0,)), ((), ())), preferred_element_type=jnp.float32)

    def scores(j, st):
        own = tags_ref[own_base + j]
        noisy = own < nclean
        limit = own % nclean + jnp.where(noisy, 0, 1)
        hidden = [jnp.where(i >= limit, NEG, 0.0).astype(jnp.float32) for i in range(nclean)]
        alone = jnp.where(noisy, 0.0, NEG).astype(jnp.float32)
        q, do = gather(q_ref, j), gather(do_ref, j)
        step = SCORE_WIDE * BLK
        for c in range(nclean // SCORE_WIDE):
            st[c * step : (c + 1) * step, :] = nt(blocks_of(ks, c, SCORE_WIDE), q)
        own_score = nt(ks[own], q)
        top = jnp.max(own_score.reshape(BLK // 8, 8, rows), axis=0) + alone
        for i in range(nclean):
            part = jnp.max(st[i * BLK : (i + 1) * BLK, :].reshape(BLK // 8, 8, rows), axis=0)
            top = jnp.maximum(top, part + hidden[i])
        top = jnp.max(top, axis=0, keepdims=True) * SCALE2
        return own, hidden, alone, q, do, own_score, top

    def weights(c, many, st, hidden, shift):
        return jnp.concatenate(
            [weight(st[i * BLK : (i + 1) * BLK, :], hidden[i] - shift) for i in range(c * many, (c + 1) * many)], axis=0
        )

    def forward(j, st, state):
        own, hidden, alone, q, do, own_score, top = state
        e = weight(own_score, alone - top)
        total = jnp.sum(e.reshape(BLK // 8, 8, rows), axis=0)
        acc = tn(vs[own], e.astype(jnp.bfloat16))
        for c in range(nclean // WEIGH_WIDE):
            e = weights(c, WEIGH_WIDE, st, hidden, top)
            total = total + jnp.sum(e.reshape(WEIGH_WIDE * BLK // 8, 8, rows), axis=0)
            acc = acc + jnp.dot(chunk_t(vt, c, WEIGH_WIDE), e.astype(jnp.bfloat16), preferred_element_type=jnp.float32)
        total = jnp.sum(total, axis=0, keepdims=True)
        attn_t = (acc / total).astype(jnp.bfloat16).astype(jnp.float32)
        delta = jnp.sum(do.astype(jnp.float32).T * attn_t, axis=0, keepdims=True)
        attn = attn_t.T.astype(jnp.bfloat16)
        for h in range(group):
            attn_ref[j * BLK : (j + 1) * BLK, h * HEAD : (h + 1) * HEAD] = attn[h * BLK : (h + 1) * BLK]
        return top + jnp.log2(total), delta

    def backward(j, st, state, top, delta):
        own, hidden, alone, q, do, own_score, unused = state

        def gradients(p, v):
            ds = (p * (nt(v, do) - delta)).astype(jnp.bfloat16)
            dvc = jnp.dot(p.astype(jnp.bfloat16), do, preferred_element_type=jnp.float32)
            dkc = jnp.dot(ds, q, preferred_element_type=jnp.float32)
            return ds, dkc, dvc

        ds, dkc, dvc = gradients(weight(own_score, alone - top), vs[own])
        dv_own[j] = dvc
        dk_own[j] = dkc
        acc = tn(ks[own], ds)
        for c in range(nclean // WIDE):
            ds, dkc, dvc = gradients(weights(c, WIDE, st, hidden, top), blocks_of(vs, c, WIDE))
            dv[pl.ds(nclean + WIDE * c, WIDE)] += dvc.reshape(WIDE, BLK, HEAD)
            dk[pl.ds(nclean + WIDE * c, WIDE)] += dkc.reshape(WIDE, BLK, HEAD)
            acc = acc + jnp.dot(chunk_t(kt, c, WIDE), ds, preferred_element_type=jnp.float32)
        dq = (acc * SCALE).T
        for h in range(group):
            dq_ref[j * BLK : (j + 1) * BLK, h * HEAD : (h + 1) * HEAD] = dq[h * BLK : (h + 1) * BLK]

    states, sums = {}, {}
    for turn in range(own_blocks + 2):
        if 0 <= turn - 2 < own_blocks:
            backward(turn - 2, st.at[turn - 2], states[turn - 2], *sums[turn - 2])
        if 0 <= turn - 1 < own_blocks:
            sums[turn - 1] = forward(turn - 1, st.at[turn - 1], states[turn - 1])
        if turn < own_blocks:
            states[turn] = scores(turn, st.at[turn])
    for far in range(SIDE):
        for near in range(SIDE):
            base = place_of(far, near) * own_blocks
            for b in range(own_blocks):
                tag = tags_ref[base + b]
                part = slice((near * own_blocks + b) * BLK, (near * own_blocks + b + 1) * BLK)
                for grad, own_grad, cols, factor in ((dk, dk_own, slice(0, HEAD), SCALE), (dv, dv_own, slice(HEAD, None), 1.0)):
                    alone = 0.0 if far or near else own_grad[b]
                    value = jnp.where(tag < nclean, alone, grad[tag])
                    outs[far][part, cols] = (value * factor).astype(jnp.bfloat16)


def attention(tags, q, do, pieces, g, group):
    tok = q.shape[0]
    nclean = tags.shape[0] // 2
    rows = group * BLK
    blocks = 2 * nclean
    return pl.pallas_call(
        functools.partial(
            attention_kernel, first=g * group, nclean=nclean, own_blocks=tok // BLK, group=group
        ),
        in_specs=[SMEM] + [VMEM] * 6,
        out_specs=[VMEM] * 6,
        out_shape=[shape((tok, group * HEAD), jnp.bfloat16), shape((tok, group * HEAD), jnp.float32)]
        + [shape(pieces[0].shape, jnp.bfloat16)] * 4,
        scratch_shapes=[
            pltpu.VMEM((blocks, BLK, HEAD), jnp.bfloat16),
            pltpu.VMEM((blocks, BLK, HEAD), jnp.bfloat16),
            pltpu.VMEM((nclean // 2, HEAD, 2 * BLK), jnp.bfloat16),
            pltpu.VMEM((nclean // 2, HEAD, 2 * BLK), jnp.bfloat16),
            pltpu.VMEM((blocks, BLK, HEAD), jnp.float32),
            pltpu.VMEM((blocks, BLK, HEAD), jnp.float32),
            pltpu.VMEM((tok // BLK, BLK, HEAD), jnp.float32),
            pltpu.VMEM((tok // BLK, BLK, HEAD), jnp.float32),
            pltpu.VMEM((tok // BLK, nclean * BLK, rows), jnp.float32),
        ],
        compiler_params=params(),
        cost_estimate=cost(6 << 30, 4 << 20),
        name="attention",
    )(tags, q, do, *pieces)


def query_back_kernel(q_ref, a_ref, b_ref, gain_ref, cos_ref, sin_ref, out_ref):
    gain, cosine, sine = gain_ref[...], cos_ref[...], sin_ref[...]
    heads = a_ref.shape[1] // HEAD
    for h in range(2 * heads):
        cols = slice(h * HEAD, (h + 1) * HEAD)
        source = (a_ref, b_ref)[h // heads]
        dy = source[:, (h % heads) * HEAD : (h % heads + 1) * HEAD]
        out_ref[:, cols] = norm_rope_back(q_ref[:, cols].astype(jnp.float32), dy, gain, cosine, sine)


def query_back(q_raw, dq0, dq1, gain, cosine, sine):
    return pl.pallas_call(
        query_back_kernel,
        grid=(1,),
        in_specs=[whole(*q_raw.shape), VMEM, VMEM, whole(*gain.shape), VMEM, VMEM],
        out_specs=whole(*q_raw.shape),
        out_shape=shape(q_raw.shape, jnp.float32),
        compiler_params=params(),
        cost_estimate=cost(1, 1),
        name="query_back",
    )(q_raw, dq0, dq1, gain, cosine, sine)


def finish_kernel(key_ref, gain_ref, cos_ref, sin_ref, a, b, c, d, keep, near, far, out_ref, dk_ref, dv_ref):
    out = keep[...].astype(jnp.float32) + near[...].astype(jnp.float32) + far[...].astype(jnp.float32)
    out_ref[...] = out.astype(jnp.bfloat16)
    gain, cosine, sine = gain_ref[...], cos_ref[...], sin_ref[...]
    for g in range(a.shape[0]):
        cols = slice(g * HEAD, (g + 1) * HEAD)
        total = a[g].astype(jnp.float32) + b[g].astype(jnp.float32)
        total += c[g].astype(jnp.float32) + d[g].astype(jnp.float32)
        x = key_ref[:, cols].astype(jnp.float32)
        dk_ref[:, cols] = norm_rope_back(x, total[:, 0:HEAD], gain, cosine, sine)
        dv_ref[:, cols] = total[:, HEAD:]


def finish(keys, gain, cosine, sine, parts, terms):
    return pl.pallas_call(
        finish_kernel,
        grid=(1,),
        in_specs=[whole(*keys.shape), whole(*gain.shape)] + [VMEM] * 9,
        out_specs=[whole(*terms[0].shape)] + [whole(*keys.shape)] * 2,
        out_shape=[shape(terms[0].shape, jnp.bfloat16)] + [shape(keys.shape, jnp.float32)] * 2,
        compiler_params=params(),
        cost_estimate=cost(0, 2 << 20),
        name="finish",
    )(keys, gain, cosine, sine, *parts, *terms)


def fold_kernel(*refs):
    parts, outs = refs[:-SIDE], refs[-SIDE:]
    rows = outs[0].shape[1]
    for g in range(len(parts) // SIDE):
        a, b, c, d = parts[SIDE * g : SIDE * g + SIDE]
        for i, out in enumerate(outs):
            part = slice(i * rows, (i + 1) * rows)
            total = a[part, :].astype(jnp.float32) + b[part, :].astype(jnp.float32)
            total += c[part, :].astype(jnp.float32) + d[part, :].astype(jnp.float32)
            out[g] = total.astype(jnp.bfloat16)


def fold(heads):
    rows, width = heads[0][0].shape
    return pl.pallas_call(
        fold_kernel,
        in_specs=[VMEM] * (SIDE * len(heads)),
        out_specs=[VMEM] * SIDE,
        out_shape=[shape((len(heads), rows // SIDE, width), jnp.bfloat16)] * SIDE,
        compiler_params=params(),
        cost_estimate=cost(0, 4 << 20),
        name="fold",
    )(*(part for parts in heads for part in parts))


def hop(value, steps, phase):
    pairs = []
    for y in range(SIDE):
        for x in range(SIDE):
            for f in range(4):
                dx, dy = (steps, 0) if (f + phase) % 2 == 0 else (0, steps)
                there = (y + dy) % SIDE * SIDE + (x + dx) % SIDE
                pairs.append(((y * SIDE + x) * 4 + f, there * 4 + f))
    return lax.ppermute(value, ("ctx", "ffn"), pairs)


def across(value, mask):
    return lax.ppermute(value, "ffn", [(s, s ^ mask) for s in range(4)])


def spread(value, phase):
    return [value] + [hop(value, k, phase) for k in range(1, SIDE)]


def collect(values, phase):
    return [values[0]] + [hop(values[k], -k, phase) for k in range(1, SIDE)]


def per_device(q_raw, keys, values, q_gain, k_gain, block_tags, w_out, d_out):
    nclean = block_tags.shape[0] // 2
    me = lax.axis_index("ffn").astype(jnp.int32)[None]
    heads = keys.shape[1] // HEAD
    group = q_raw.shape[1] // keys.shape[1]
    q_gain, k_gain = q_gain[None, :], k_gain[None, :]
    table = jnp.asarray(angle_table(nclean))

    kv, cosine, sine = key_prep(block_tags, keys, values, k_gain, table, heads)
    near = spread(kv, 0)
    q = query_prep(q_raw, q_gain, cosine, sine)
    lines = [jnp.concatenate([part[g] for part in near], axis=0) for g in range(heads)]
    lines[0], q = lax.optimization_barrier((lines[0], q))
    far = across(d_out, 2)
    half = far.shape[0] // 2
    d_pieces = [d_out, across(d_out, 1), far, across(far[:half], 1), across(far[half:], 1)]
    do = d_attn_product(me, d_pieces, w_out)

    pieces = []
    for g in range(heads):
        line = lines[g]
        if g:
            line, do, pieces[g - 1] = lax.optimization_barrier((line, do, pieces[g - 1]))
        pieces.append(spread(line, 1))

    attn, dq, sums = [], [], []
    for g in range(heads):
        results = attention(block_tags, q, do, pieces[g], g, group)
        if g:
            results, sums[g - 1] = lax.optimization_barrier((results, sums[g - 1]))
        attn_g, dq_g, *grads = results
        attn.append(attn_g)
        dq.append(dq_g)
        sums.append(collect(grads, 1))
    far_a, far_b, keep_far, near, keep_near = out_product(me, attn[0], attn[1], w_out)
    far = jnp.concatenate([across(far_a, 1), across(far_b, 1)], axis=0)
    far = (keep_far.astype(jnp.float32) + far.astype(jnp.float32)).astype(jnp.bfloat16)
    shares, far, near = lax.optimization_barrier((fold(sums), far, near))
    parts = collect(shares, 0)
    terms = [keep_near, across(near, 1), across(far, 2)]
    d_q = query_back(q_raw, dq[0], dq[1], q_gain, cosine, sine)
    attn_out, key_gradient, value_gradient = finish(keys, k_gain, cosine, sine, parts, terms)
    return attn_out, d_q, key_gradient, value_gradient


def solution(mesh):
    split = P(("dp", "ctx"), "ffn")
    return jax.shard_map(
        per_device,
        mesh=mesh,
        in_specs=(split, split, split, P(), P(), P("dp"), P("ffn", None), split),
        out_specs=(split,) * 4,
        check_vma=False,
    )
```

```python
import functools

import jax
import jax.numpy as jnp
import numpy as np
from jax import lax
from jax.experimental import pallas as pl
from jax.experimental.pallas import tpu as pltpu
from jax.sharding import PartitionSpec as P

HEAD = 128
BLK = 64
ROPE_BASE = 1000000.0
EPS = 1e-06
NEG = -1e30
SCALE = HEAD ** (-0.5)
SCALE2 = SCALE * 1.4426950408889634
WIDE = 8
SCORE_WIDE = 4
WEIGH_WIDE = 16
SIDE = 4
VMEM = pl.BlockSpec(memory_space=pltpu.VMEM)
SMEM = pl.BlockSpec(memory_space=pltpu.SMEM)
HBM = pl.BlockSpec(memory_space=pltpu.HBM)
LIMIT = 32 * 1024 * 1024


def shape(dims, dtype):
    return jax.ShapeDtypeStruct(dims, dtype)


def params(limit=LIMIT):
    return pltpu.CompilerParams(vmem_limit_bytes=limit)


def cost(flops, nbytes):
    return pl.CostEstimate(flops=flops, bytes_accessed=nbytes, transcendentals=0)


def angle_table(blocks):
    freq = ROPE_BASE ** (-(np.arange(HEAD // 2) * 2.0 / HEAD))
    freq = np.concatenate([freq, freq])[None, :]
    inner = np.arange(BLK)[:, None] * freq
    outer = (np.arange(blocks) * BLK)[:, None] * freq
    return np.concatenate([np.cos(inner), np.sin(inner), np.cos(outer), np.sin(outer)]).astype(np.float32)


def half_sign():
    lane = lax.broadcasted_iota(jnp.int32, (1, HEAD), 1)
    return jnp.where(lane < HEAD // 2, -1.0, 1.0).astype(jnp.float32)


def block_angles(table_ref, index, blocks):
    c_in, s_in = table_ref[0:BLK, :], table_ref[BLK : 2 * BLK, :]
    c_out = table_ref[pl.ds(2 * BLK + index, 1), :]
    s_out = table_ref[pl.ds(2 * BLK + blocks + index, 1), :]
    return c_in * c_out - s_in * s_out, s_in * c_out + c_in * s_out


def norm_rope(x, gain, cosine, sine_signed):
    normed = x * lax.rsqrt(jnp.mean(x * x, axis=-1, keepdims=True) + EPS) * gain
    return normed * cosine + pltpu.roll(normed, HEAD // 2, 1) * sine_signed


def norm_rope_back(x, dy, gain, cosine, sine_signed):
    inv = lax.rsqrt(jnp.mean(x * x, axis=-1, keepdims=True) + EPS)
    dn = (dy * cosine + pltpu.roll(dy * sine_signed, HEAD // 2, 1)) * gain
    inner = jnp.mean(x * dn, axis=-1, keepdims=True)
    return inv * dn - x * (inv * inv * inv * inner)


def whole(*dims):
    return pl.BlockSpec(dims, lambda i: (0,) * len(dims))


def key_kernel(
    tags_ref, key_hbm, value_hbm, gain_hbm, table_hbm, out_ref, cos_ref, sin_ref, key_ref, gain_ref, table_ref, sems, *, blocks
):
    heads, tok = out_ref.shape[0], key_ref.shape[0]
    copies = [
        pltpu.make_async_copy(source, dest, sems.at[i])
        for i, (source, dest) in enumerate(((key_hbm, key_ref), (gain_hbm, gain_ref), (table_hbm, table_ref)))
    ]
    copies += [
        pltpu.make_async_copy(value_hbm.at[:, pl.ds(g * HEAD, HEAD)], out_ref.at[g, :, pl.ds(HEAD, HEAD)], sems.at[3 + g])
        for g in range(heads)
    ]
    for copy in copies:
        copy.start()
    for copy in copies[:3]:
        copy.wait()
    gain, sign = gain_ref[...], half_sign()
    own_blocks = tok // BLK
    base = place_of(0, 0) * own_blocks
    for j in range(own_blocks):
        rows = slice(j * BLK, (j + 1) * BLK)
        cosine, sine = block_angles(table_ref, tags_ref[base + j] % blocks, blocks)
        sine = sine * sign
        cos_ref[rows, :] = cosine
        sin_ref[rows, :] = sine
        for g in range(heads):
            x = key_ref[rows, g * HEAD : (g + 1) * HEAD].astype(jnp.float32)
            out_ref[g, rows, 0:HEAD] = norm_rope(x, gain, cosine, sine).astype(jnp.bfloat16)
    for copy in copies[3:]:
        copy.wait()


def key_prep(tags, keys, values, gain, table, heads):
    tok = keys.shape[0]
    blocks = (table.shape[0] - 2 * BLK) // 2
    return pl.pallas_call(
        functools.partial(key_kernel, blocks=blocks),
        in_specs=[SMEM] + [HBM] * 4,
        out_specs=[VMEM] * 3,
        out_shape=[shape((heads, tok, 2 * HEAD), jnp.bfloat16)] + [shape((tok, HEAD), jnp.float32)] * 2,
        scratch_shapes=[
            pltpu.VMEM(keys.shape, keys.dtype),
            pltpu.VMEM(gain.shape, gain.dtype),
            pltpu.VMEM(table.shape, table.dtype),
            pltpu.SemaphoreType.DMA((3 + heads,)),
        ],
        compiler_params=params(63 * 1024 * 1024),
        cost_estimate=cost(0, 1 << 20),
        name="key_prep",
    )(tags, keys, values, gain, table)


def query_kernel(q_ref, gain_ref, cos_ref, sin_ref, out_ref):
    gain, cosine, sine = gain_ref[...], cos_ref[...], sin_ref[...]
    for h in range(q_ref.shape[1] // HEAD):
        cols = slice(h * HEAD, (h + 1) * HEAD)
        x = q_ref[:, cols].astype(jnp.float32)
        out_ref[:, cols] = norm_rope(x, gain, cosine, sine).astype(jnp.bfloat16)


def query_prep(q_raw, gain, cosine, sine):
    return pl.pallas_call(
        query_kernel,
        grid=(1,),
        in_specs=[whole(*q_raw.shape), whole(*gain.shape), whole(*cosine.shape), whole(*sine.shape)],
        out_specs=whole(*q_raw.shape),
        out_shape=shape(q_raw.shape, jnp.bfloat16),
        compiler_params=params(63 * 1024 * 1024),
        cost_estimate=cost(0, 4 << 20),
        name="query_prep",
    )(q_raw, gain, cosine, sine)


def d_attn_kernel(me_ref, p0, p1, p2, p3a, p3b, w_ref, out_ref, acc):
    k = pl.program_id(0)

    def product(piece):
        return lax.dot_general(piece, w_ref[...], (((1,), (1,)), ((), ())), preferred_element_type=jnp.float32)

    @pl.when(k == 0)
    def _():
        acc[...] = product(p0[...])

    @pl.when(k == 1)
    def _():
        acc[...] += product(p1[...])

    @pl.when(k == 2)
    def _():
        acc[...] += product(p2[...])

    @pl.when(k == 3)
    def _():
        both = jnp.concatenate([p3a[...], p3b[...]], axis=0)
        out_ref[...] = (acc[...] + product(both)).astype(jnp.bfloat16)


def d_attn_product(me, pieces, w_out):
    tok, width = pieces[0].shape
    feats = w_out.shape[0]
    place = lambda k, me: (0, 0)
    return pl.pallas_call(
        d_attn_kernel,
        grid_spec=pltpu.PrefetchScalarGridSpec(
            num_scalar_prefetch=1,
            grid=(4,),
            in_specs=[pl.BlockSpec(piece.shape, place) for piece in pieces]
            + [pl.BlockSpec((feats, width), lambda k, me: (0, me[0] ^ k))],
            out_specs=pl.BlockSpec((tok, feats), place),
            scratch_shapes=[pltpu.VMEM((tok, feats), jnp.float32)],
        ),
        out_shape=shape((tok, feats), jnp.bfloat16),
        compiler_params=params(),
        cost_estimate=cost(1, 1),
        name="d_attn_product",
    )(me, *pieces, w_out)


def out_kernel(me_ref, a0_ref, a1_ref, w_ref, far_a, far_b, keep_far, near, keep_near):
    k = pl.program_id(0)
    half = a0_ref.shape[1]
    term = jnp.dot(a0_ref[...], w_ref[0:half, :], preferred_element_type=jnp.float32)
    term += jnp.dot(a1_ref[...], w_ref[half:, :], preferred_element_type=jnp.float32)
    term = term.astype(jnp.bfloat16)
    rows = far_a.shape[0]

    @pl.when(k == 0)
    def _():
        far_a[...] = term[:rows]
        far_b[...] = term[rows:]

    for i, out in enumerate((keep_far, near, keep_near)):

        @pl.when(k == i + 1)
        def _(out=out):
            out[...] = term


def out_product(me, a0, a1, w_out):
    tok = a0.shape[0]
    feats, wide = w_out.shape
    width = wide // 4
    place = lambda k, me: (0, 0)
    dims = [(tok // 2, width)] * 2 + [(tok, width)] * 3
    return pl.pallas_call(
        out_kernel,
        grid_spec=pltpu.PrefetchScalarGridSpec(
            num_scalar_prefetch=1,
            grid=(4,),
            in_specs=[pl.BlockSpec(a0.shape, place)] * 2
            + [pl.BlockSpec((feats, width), lambda k, me: (0, me[0] ^ (3 - k)))],
            out_specs=[pl.BlockSpec(d, place) for d in dims],
        ),
        out_shape=[shape(d, jnp.bfloat16) for d in dims],
        compiler_params=params(),
        cost_estimate=cost(1, 1),
        name="out_product",
    )(me, a0, a1, w_out)


def place_of(far, near):
    here = lax.axis_index("ctx")
    first = lax.axis_index("ffn") % 2 == 0
    dx = jnp.where(first, near, far)
    dy = jnp.where(first, far, near)
    return (here // SIDE - dy + SIDE) % SIDE * SIDE + (here % SIDE - dx + SIDE) % SIDE


def attention_kernel(tags_ref, q_ref, do_ref, *refs, first, nclean, own_blocks, group):
    pieces, (attn_ref, dq_ref), outs = refs[0:4], refs[4:6], refs[6:10]
    ks, vs, kt, vt, dk, dv, dk_own, dv_own, st = refs[10:]
    rows = group * BLK
    own_base = place_of(0, 0) * own_blocks
    for far in range(SIDE):
        for near in range(SIDE):
            base = place_of(far, near) * own_blocks
            for b in range(own_blocks):
                tag = tags_ref[base + b]
                part = slice((near * own_blocks + b) * BLK, (near * own_blocks + b + 1) * BLK)
                ks[tag] = pieces[far][part, 0:HEAD]
                vs[tag] = pieces[far][part, HEAD:]

    def flip(ref, pair):
        return ref[pl.ds(nclean + 2 * pair, 2)].reshape(2 * BLK, HEAD).astype(jnp.float32).T.astype(jnp.bfloat16)

    def blocks_of(ref, c, many):
        return ref[pl.ds(nclean + many * c, many)].reshape(many * BLK, HEAD)

    def chunk_t(ref, c, many):
        return jnp.concatenate([ref[many // 2 * c + i] for i in range(many // 2)], axis=1)

    for pair in range(nclean // 2):
        kt[pair] = flip(ks, pair)
        vt[pair] = flip(vs, pair)
    for grad in (dk, dv):
        grad[pl.ds(nclean, nclean)] = jnp.zeros((nclean, BLK, HEAD), jnp.float32)

    def gather(ref, j):
        return jnp.concatenate(
            [ref[j * BLK : (j + 1) * BLK, (first + h) * HEAD : (first + h + 1) * HEAD] for h in range(group)], axis=0
        )

    def weight(score, bias):
        return jnp.exp2(score * SCALE2 + bias)

    def nt(left, right):
        return lax.dot_general(left, right, (((1,), (1,)), ((), ())), preferred_element_type=jnp.float32)

    def tn(left, right):
        return lax.dot_general(left, right, (((0,), (0,)), ((), ())), preferred_element_type=jnp.float32)

    def scores(j, st):
        own = tags_ref[own_base + j]
        noisy = own < nclean
        limit = own % nclean + jnp.where(noisy, 0, 1)
        hidden = [jnp.where(i >= limit, NEG, 0.0).astype(jnp.float32) for i in range(nclean)]
        alone = jnp.where(noisy, 0.0, NEG).astype(jnp.float32)
        q, do = gather(q_ref, j), gather(do_ref, j)
        step = SCORE_WIDE * BLK
        for c in range(nclean // SCORE_WIDE):
            st[c * step : (c + 1) * step, :] = nt(blocks_of(ks, c, SCORE_WIDE), q)
        own_score = nt(ks[own], q)
        top = jnp.max(own_score.reshape(BLK // 8, 8, rows), axis=0) + alone
        for i in range(nclean):
            part = jnp.max(st[i * BLK : (i + 1) * BLK, :].reshape(BLK // 8, 8, rows), axis=0)
            top = jnp.maximum(top, part + hidden[i])
        top = jnp.max(top, axis=0, keepdims=True) * SCALE2
        return own, hidden, alone, q, do, own_score, top

    def weights(c, many, st, hidden, shift):
        return jnp.concatenate(
            [weight(st[i * BLK : (i + 1) * BLK, :], hidden[i] - shift) for i in range(c * many, (c + 1) * many)], axis=0
        )

    def forward(j, st, state):
        own, hidden, alone, q, do, own_score, top = state
        e = weight(own_score, alone - top)
        total = jnp.sum(e.reshape(BLK // 8, 8, rows), axis=0)
        acc = tn(vs[own], e.astype(jnp.bfloat16))
        for c in range(nclean // WEIGH_WIDE):
            e = weights(c, WEIGH_WIDE, st, hidden, top)
            total = total + jnp.sum(e.reshape(WEIGH_WIDE * BLK // 8, 8, rows), axis=0)
            acc = acc + jnp.dot(chunk_t(vt, c, WEIGH_WIDE), e.astype(jnp.bfloat16), preferred_element_type=jnp.float32)
        total = jnp.sum(total, axis=0, keepdims=True)
        attn_t = (acc / total).astype(jnp.bfloat16).astype(jnp.float32)
        delta = jnp.sum(do.astype(jnp.float32).T * attn_t, axis=0, keepdims=True)
        attn = attn_t.T.astype(jnp.bfloat16)
        for h in range(group):
            attn_ref[j * BLK : (j + 1) * BLK, h * HEAD : (h + 1) * HEAD] = attn[h * BLK : (h + 1) * BLK]
        return top + jnp.log2(total), delta

    def backward(j, st, state, top, delta):
        own, hidden, alone, q, do, own_score, unused = state

        def gradients(p, v):
            ds = (p * (nt(v, do) - delta)).astype(jnp.bfloat16)
            dvc = jnp.dot(p.astype(jnp.bfloat16), do, preferred_element_type=jnp.float32)
            dkc = jnp.dot(ds, q, preferred_element_type=jnp.float32)
            return ds, dkc, dvc

        ds, dkc, dvc = gradients(weight(own_score, alone - top), vs[own])
        dv_own[j] = dvc
        dk_own[j] = dkc
        acc = tn(ks[own], ds)
        for c in range(nclean // WIDE):
            ds, dkc, dvc = gradients(weights(c, WIDE, st, hidden, top), blocks_of(vs, c, WIDE))
            dv[pl.ds(nclean + WIDE * c, WIDE)] += dvc.reshape(WIDE, BLK, HEAD)
            dk[pl.ds(nclean + WIDE * c, WIDE)] += dkc.reshape(WIDE, BLK, HEAD)
            acc = acc + jnp.dot(chunk_t(kt, c, WIDE), ds, preferred_element_type=jnp.float32)
        dq = (acc * SCALE).T
        for h in range(group):
            dq_ref[j * BLK : (j + 1) * BLK, h * HEAD : (h + 1) * HEAD] = dq[h * BLK : (h + 1) * BLK]

    states, sums = {}, {}
    for turn in range(own_blocks + 2):
        if 0 <= turn - 2 < own_blocks:
            backward(turn - 2, st.at[turn - 2], states[turn - 2], *sums[turn - 2])
        if 0 <= turn - 1 < own_blocks:
            sums[turn - 1] = forward(turn - 1, st.at[turn - 1], states[turn - 1])
        if turn < own_blocks:
            states[turn] = scores(turn, st.at[turn])
    for far in range(SIDE):
        for near in range(SIDE):
            base = place_of(far, near) * own_blocks
            for b in range(own_blocks):
                tag = tags_ref[base + b]
                part = slice((near * own_blocks + b) * BLK, (near * own_blocks + b + 1) * BLK)
                for grad, own_grad, cols, factor in ((dk, dk_own, slice(0, HEAD), SCALE), (dv, dv_own, slice(HEAD, None), 1.0)):
                    alone = 0.0 if far or near else own_grad[b]
                    value = jnp.where(tag < nclean, alone, grad[tag])
                    outs[far][part, cols] = (value * factor).astype(jnp.bfloat16)


def attention(tags, q, do, pieces, g, group):
    tok = q.shape[0]
    nclean = tags.shape[0] // 2
    rows = group * BLK
    blocks = 2 * nclean
    return pl.pallas_call(
        functools.partial(
            attention_kernel, first=g * group, nclean=nclean, own_blocks=tok // BLK, group=group
        ),
        in_specs=[SMEM] + [VMEM] * 6,
        out_specs=[VMEM] * 6,
        out_shape=[shape((tok, group * HEAD), jnp.bfloat16), shape((tok, group * HEAD), jnp.float32)]
        + [shape(pieces[0].shape, jnp.bfloat16)] * 4,
        scratch_shapes=[
            pltpu.VMEM((blocks, BLK, HEAD), jnp.bfloat16),
            pltpu.VMEM((blocks, BLK, HEAD), jnp.bfloat16),
            pltpu.VMEM((nclean // 2, HEAD, 2 * BLK), jnp.bfloat16),
            pltpu.VMEM((nclean // 2, HEAD, 2 * BLK), jnp.bfloat16),
            pltpu.VMEM((blocks, BLK, HEAD), jnp.float32),
            pltpu.VMEM((blocks, BLK, HEAD), jnp.float32),
            pltpu.VMEM((tok // BLK, BLK, HEAD), jnp.float32),
            pltpu.VMEM((tok // BLK, BLK, HEAD), jnp.float32),
            pltpu.VMEM((tok // BLK, nclean * BLK, rows), jnp.float32),
        ],
        compiler_params=params(),
        cost_estimate=cost(6 << 30, 4 << 20),
        name="attention",
    )(tags, q, do, *pieces)


def query_back_kernel(q_ref, a_ref, b_ref, gain_ref, cos_ref, sin_ref, out_ref):
    gain, cosine, sine = gain_ref[...], cos_ref[...], sin_ref[...]
    heads = a_ref.shape[1] // HEAD
    for h in range(2 * heads):
        cols = slice(h * HEAD, (h + 1) * HEAD)
        source = (a_ref, b_ref)[h // heads]
        dy = source[:, (h % heads) * HEAD : (h % heads + 1) * HEAD]
        out_ref[:, cols] = norm_rope_back(q_ref[:, cols].astype(jnp.float32), dy, gain, cosine, sine)


def query_back(q_raw, dq0, dq1, gain, cosine, sine):
    return pl.pallas_call(
        query_back_kernel,
        grid=(1,),
        in_specs=[whole(*q_raw.shape), VMEM, VMEM, whole(*gain.shape), VMEM, VMEM],
        out_specs=whole(*q_raw.shape),
        out_shape=shape(q_raw.shape, jnp.float32),
        compiler_params=params(),
        cost_estimate=cost(1, 1),
        name="query_back",
    )(q_raw, dq0, dq1, gain, cosine, sine)


def finish_kernel(key_ref, gain_ref, cos_ref, sin_ref, a, b, c, d, keep, near, far, out_ref, dk_ref, dv_ref):
    out = keep[...].astype(jnp.float32) + near[...].astype(jnp.float32) + far[...].astype(jnp.float32)
    out_ref[...] = out.astype(jnp.bfloat16)
    gain, cosine, sine = gain_ref[...], cos_ref[...], sin_ref[...]
    for g in range(a.shape[0]):
        cols = slice(g * HEAD, (g + 1) * HEAD)
        total = a[g].astype(jnp.float32) + b[g].astype(jnp.float32)
        total += c[g].astype(jnp.float32) + d[g].astype(jnp.float32)
        x = key_ref[:, cols].astype(jnp.float32)
        dk_ref[:, cols] = norm_rope_back(x, total[:, 0:HEAD], gain, cosine, sine)
        dv_ref[:, cols] = total[:, HEAD:]


def finish(keys, gain, cosine, sine, parts, terms):
    return pl.pallas_call(
        finish_kernel,
        grid=(1,),
        in_specs=[whole(*keys.shape), whole(*gain.shape)] + [VMEM] * 9,
        out_specs=[whole(*terms[0].shape)] + [whole(*keys.shape)] * 2,
        out_shape=[shape(terms[0].shape, jnp.bfloat16)] + [shape(keys.shape, jnp.float32)] * 2,
        compiler_params=params(),
        cost_estimate=cost(0, 2 << 20),
        name="finish",
    )(keys, gain, cosine, sine, *parts, *terms)


def fold_kernel(*refs):
    parts, outs = refs[:-SIDE], refs[-SIDE:]
    rows = outs[0].shape[1]
    for g in range(len(parts) // SIDE):
        a, b, c, d = parts[SIDE * g : SIDE * g + SIDE]
        for i, out in enumerate(outs):
            part = slice(i * rows, (i + 1) * rows)
            total = a[part, :].astype(jnp.float32) + b[part, :].astype(jnp.float32)
            total += c[part, :].astype(jnp.float32) + d[part, :].astype(jnp.float32)
            out[g] = total.astype(jnp.bfloat16)


def fold(heads):
    rows, width = heads[0][0].shape
    return pl.pallas_call(
        fold_kernel,
        in_specs=[VMEM] * (SIDE * len(heads)),
        out_specs=[VMEM] * SIDE,
        out_shape=[shape((len(heads), rows // SIDE, width), jnp.bfloat16)] * SIDE,
        compiler_params=params(),
        cost_estimate=cost(0, 4 << 20),
        name="fold",
    )(*(part for parts in heads for part in parts))


def hop(value, steps, phase):
    pairs = []
    for y in range(SIDE):
        for x in range(SIDE):
            for f in range(4):
                dx, dy = (steps, 0) if (f + phase) % 2 == 0 else (0, steps)
                there = (y + dy) % SIDE * SIDE + (x + dx) % SIDE
                pairs.append(((y * SIDE + x) * 4 + f, there * 4 + f))
    return lax.ppermute(value, ("ctx", "ffn"), pairs)


def across(value, mask):
    return lax.ppermute(value, "ffn", [(s, s ^ mask) for s in range(4)])


def spread(value, phase):
    return [value] + [hop(value, k, phase) for k in range(1, SIDE)]


def collect(values, phase):
    return [values[0]] + [hop(values[k], -k, phase) for k in range(1, SIDE)]


def per_device(q_raw, keys, values, q_gain, k_gain, block_tags, w_out, d_out):
    nclean = block_tags.shape[0] // 2
    me = lax.axis_index("ffn").astype(jnp.int32)[None]
    heads = keys.shape[1] // HEAD
    group = q_raw.shape[1] // keys.shape[1]
    q_gain, k_gain = q_gain[None, :], k_gain[None, :]
    table = jnp.asarray(angle_table(nclean))

    kv, cosine, sine = key_prep(block_tags, keys, values, k_gain, table, heads)
    near = spread(kv, 0)
    q = query_prep(q_raw, q_gain, cosine, sine)
    lines = [jnp.concatenate([part[g] for part in near], axis=0) for g in range(heads)]
    lines[0], q = lax.optimization_barrier((lines[0], q))
    far = across(d_out, 2)
    half = far.shape[0] // 2
    d_pieces = [d_out, across(d_out, 1), far, across(far[:half], 1), across(far[half:], 1)]
    do = d_attn_product(me, d_pieces, w_out)

    pieces = []
    for g in range(heads):
        line = lines[g]
        if g:
            line, do, pieces[g - 1] = lax.optimization_barrier((line, do, pieces[g - 1]))
        pieces.append(spread(line, 1))

    attn, dq, sums = [], [], []
    for g in range(heads):
        results = attention(block_tags, q, do, pieces[g], g, group)
        if g:
            shares = out_product(me, attn[0], results[0], w_out)
            results, shares, sums[g - 1] = lax.optimization_barrier((results, shares, sums[g - 1]))
        attn_g, dq_g, *grads = results
        attn.append(attn_g)
        dq.append(dq_g)
        sums.append(collect(grads, 1))
    far_a, far_b, keep_far, near, keep_near = shares
    far = jnp.concatenate([across(far_a, 1), across(far_b, 1)], axis=0)
    far = (keep_far.astype(jnp.float32) + far.astype(jnp.float32)).astype(jnp.bfloat16)
    terms = [keep_near, across(near, 1), across(far, 2)]
    parts = collect(fold(sums), 0)
    d_q = query_back(q_raw, dq[0], dq[1], q_gain, cosine, sine)
    attn_out, key_gradient, value_gradient = finish(keys, k_gain, cosine, sine, parts, terms)
    return attn_out, d_q, key_gradient, value_gradient


def solution(mesh):
    split = P(("dp", "ctx"), "ffn")
    return jax.shard_map(
        per_device,
        mesh=mesh,
        in_specs=(split, split, split, P(), P(), P("dp"), P("ffn", None), split),
        out_specs=(split,) * 4,
        check_vma=False,
    )
```
